512 devices in a mesh: gx: 16 (over x, z_hi, core), gy: 4 (over y), gz: 8 (over z_lo).
Axes of the slice: x: 4, y: 4, z: 16 (z_hi: 2, z_lo: 8; z = z_hi * 8 + z_lo), core: 2. Of those that a mesh axis runs over, the one named last changes fastest.
Arguments:
- wave: float32 [256, 128, 1024], P('gx', 'gy', 'gz'), may hold values from -7 to 7
- external: float32 [256, 128, 1024], P('gx', 'gy', 'gz'), may hold values from 0 to 2
- weights: float32 [3, 17], replicated, may hold values from 0.02 to 0.1
Outputs:
- wave_next: float32 [256, 128, 1024], P('gx', 'gy', 'gz')
- correlation: float32 [256, 128, 1024], P('gx', 'gy', 'gz')
The draws below stay inside these ranges and needn't reach their ends.
All inputs are finite; a program needn't handle non-finite values.
Results may differ from the reference program's by a relative error of at most 0.00029.
Values sent between devices are 32-bit elements; how exact they have to be, the bound alone decides.
No kernel may reach another device: no remote copies, remote signals or barrier semaphores. Data moves between devices by JAX's collectives and lax.ppermute only.
A program may use at most 64 MiB of HBM per device.

```python
import math
import jax
import jax.numpy as jnp
from jax import lax

CX = 16
CY = 32
CZ = 128
SUBSTEPS = 3
NX = 256
NY = 128
NZ = 1024


def tile_levels(key, low, high):
    level_key, shift_key = jax.random.split(key)
    counts = (NX // CX, NY // CY, NZ // CZ)
    logs = jax.random.uniform(level_key, counts, jnp.float32, jnp.log(low), jnp.log(high))
    levels = jnp.exp(logs)
    levels = jnp.repeat(levels, CX, axis=0)
    levels = jnp.repeat(levels, CY, axis=1)
    levels = jnp.repeat(levels, CZ, axis=2)
    shifts = jax.random.randint(shift_key, (3,), 0, 4)
    levels = jnp.roll(levels, shifts[0], axis=0)
    levels = jnp.roll(levels, shifts[1], axis=1)
    levels = jnp.roll(levels, shifts[2], axis=2)
    return levels


def draw_wave(key, part):
    first = jax.random.fold_in(key, 0)
    rise = 1.0 + 0.732 * jnp.arange(NX, dtype=jnp.float32) / max(NX - 1, 1)
    amplitude = tile_levels(jax.random.fold_in(key, 11), 0.45, 1.1)
    rough = jnp.clip(jax.random.normal(first, (NX, NY, NZ), jnp.float32), -4.0, 4.0)
    values = rough * rise[:, None, None] * amplitude
    return jnp.clip(values, -7.0, 7.0).astype(jnp.float32)


def draw_external(key, part):
    first, second = jax.random.split(jax.random.fold_in(key, 23))
    levels = tile_levels(first, 0.15, 1.0)
    rough = jnp.exp(jax.random.uniform(second, (NX, NY, NZ), jnp.float32, jnp.log(0.5), jnp.log(2.0)))
    return jnp.clip(levels * rough, 0.0, 2.0).astype(jnp.float32)


def setup_inputs(seed: int = 0) -> dict:
    key_of = jax.random.split(jax.random.key(seed), 4)
    return {
        "wave": draw_wave(jax.random.fold_in(key_of[3], 71), 0),
        "external": draw_external(jax.random.fold_in(key_of[3], 71), 0),
        "weights": jnp.clip(jnp.exp(jax.random.uniform(key_of[2], (3, 17), jnp.float32, math.log(0.02), math.log(0.1))), 0.02, 0.1),
    }


LAP_COEF = (-205.0 / 72.0, 8.0 / 5.0, -1.0 / 5.0, 8.0 / 315.0, -1.0 / 560.0)

def smear(field, weights, flip):
    for dim in range(3):
        length = field.shape[dim]
        widths = [(0, 0), (0, 0), (0, 0)]
        widths[dim] = (8, 8)
        padded = jnp.pad(field, widths)
        total = jnp.zeros_like(field)
        for tap in range(17):
            coef = weights[dim, 16 - tap] if flip else weights[dim, tap]
            total = total + coef * lax.slice_in_dim(padded, tap, tap + length, axis=dim)
        field = total
    return field

def laplace(field):
    padded = jnp.pad(field, 4)
    total = 3.0 * LAP_COEF[0] * field
    for dim in range(3):
        length = field.shape[dim]
        inner = [slice(4, -4), slice(4, -4), slice(4, -4)]
        for step in range(1, 5):
            upper = list(inner)
            lower = list(inner)
            upper[dim] = slice(4 + step, 4 + step + length)
            lower[dim] = slice(4 - step, 4 - step + length)
            total = total + LAP_COEF[step] * (padded[tuple(upper)] + padded[tuple(lower)])
    return total

def reference(wave, external, weights):
    density = wave * wave
    coarse = smear(density, weights, False)
    source = -1.0 * density * coarse + 0.5 * density * coarse * coarse
    correlation = -0.5 * coarse * coarse + 0.5 / 3.0 * coarse * coarse * coarse + smear(source, weights, True)
    potential = correlation + external
    psi = wave
    for step in range(SUBSTEPS):
        psi = psi - 0.08 * (-0.5 * laplace(psi) + potential * psi)
    total = jnp.sum(psi * psi)
    wave_next = psi * lax.rsqrt(total / (NX * NY * NZ) + 1e-06)
    return (wave_next, correlation)
```

```python
import jax
import jax.numpy as jnp
from jax import lax
from jax.sharding import Mesh
from jax.sharding import PartitionSpec as P

SUBSTEPS = 3
RINGS = (("gx_1", "gx_2", "gz"), ("gx_0", "gy"))
GX = ("gx_0", "gx_1", "gx_2")


LAP_COEF = (-205.0 / 72.0, 8.0 / 5.0, -1.0 / 5.0, 8.0 / 315.0, -1.0 / 560.0)
FORMS = ("jyz,ji->iyz", "xjz,ji->xiz", "xyj,ji->xyi")


def with_halo(cells, sides, width):
    for axis, dim in sides:
        count = lax.axis_size(axis)
        ends = count - 1
        head = lax.slice_in_dim(cells, 0, width, axis=dim)
        tail = lax.slice_in_dim(cells, cells.shape[dim] - width, cells.shape[dim], axis=dim)
        cells = jnp.concatenate(
            [
                lax.ppermute(tail, axis, [(i, (i + 1) % count) for i in range(ends)]),
                cells,
                lax.ppermute(head, axis, [((i + 1) % count, i) for i in range(ends)]),
            ],
            axis=dim,
        )
    return cells


def with_halo_2(array, sides, width):
    edges = {}
    for axis, dim in sides:
        size, length = (lax.axis_size(axis), array.shape[dim])
        up = [(i, (i + 1) % size) for i in range(size - 1)]
        last = lax.slice_in_dim(array, length - width, length, axis=dim)
        leading = lax.slice_in_dim(array, 0, width, axis=dim)
        edges[dim] = (
            lax.ppermute(last, axis, up),
            lax.ppermute(leading, axis, [(b, a) for a, b in up]),
        )
    done = []
    for _, dim in sides:
        low, high = edges[dim]
        around = [(width, width) if d in done else (0, 0) for d in range(array.ndim)]
        array = jnp.concatenate([jnp.pad(low, around), array, jnp.pad(high, around)], axis=dim)
        done.append(dim)
    return array


def spread_sum(row, groups):
    for axes in groups:
        count = lax.axis_size(axes)
        copies = jnp.broadcast_to(row[None], (count, *row.shape))
        row = jnp.sum(lax.all_to_all(copies, axes, 0, 0, tiled=True), axis=0)
    return jnp.sum(row)


def band_matrix(row, size_in, flip):
    size_out = size_in - 16
    rows_at = lax.broadcasted_iota(jnp.int32, (size_in, size_out), 0)
    cols_at = lax.broadcasted_iota(jnp.int32, (size_in, size_out), 1)
    offset = rows_at - cols_at
    if flip:
        offset = 16 - offset
    taps = jnp.arange(17, dtype=jnp.int32)
    return jnp.sum(jnp.where(offset[:, :, None] == taps, row, 0.0), axis=2)


def smear(padded, weights, flip):
    for dim in range(3):
        matrix = band_matrix(weights[dim], padded.shape[dim], flip)
        padded = jnp.einsum(FORMS[dim], padded, matrix, precision=lax.Precision.HIGHEST)
    return padded


def trim(field, margin):
    return field[margin:-margin, margin:-margin, margin:-margin]


def laplace(padded):
    center = trim(padded, 4)
    total = 3.0 * LAP_COEF[0] * center
    for dim in range(3):
        length = center.shape[dim]
        for step in range(1, 5):
            upper = [slice(4, -4), slice(4, -4), slice(4, -4)]
            lower = [slice(4, -4), slice(4, -4), slice(4, -4)]
            upper[dim] = slice(4 + step, 4 + step + length)
            lower[dim] = slice(4 - step, 4 - step + length)
            total = total + LAP_COEF[step] * (padded[tuple(upper)] + padded[tuple(lower)])
    return total


def shards(wave, external, weights):
    wide = with_halo(wave, ((GX, 0), ("gy", 1), ("gz", 2)), 16)
    density_wide = wide * wide
    coarse_wide = smear(density_wide, weights, False)
    density_near = trim(density_wide, 8)
    source_near = -1.0 * density_near * coarse_wide + 0.5 * density_near * coarse_wide * coarse_wide
    coarse = trim(coarse_wide, 8)
    correlation = (
        -0.5 * coarse * coarse
        + 0.5 / 3.0 * coarse * coarse * coarse
        + smear(source_near, weights, True)
    )
    potential = correlation + external
    psi = wave
    for step in range(SUBSTEPS):
        near = with_halo_2(psi, ((GX, 0), ("gy", 1), ("gz", 2)), 4)
        psi = psi - 0.08 * (-0.5 * laplace(near) + potential * psi)
    total = spread_sum(jnp.sum(psi * psi, axis=(0, 1))[None], RINGS)
    count = float(psi.size * lax.axis_size(GX) * lax.axis_size("gy") * lax.axis_size("gz"))
    wave_next = psi * lax.rsqrt(total / count + 1e-06)
    return (wave_next, correlation)


def solution(mesh):
    torus = Mesh(
        mesh.devices.reshape(4, 2, 2, mesh.shape["gy"], mesh.shape["gz"]),
        ("gx_0", "gx_1", "gx_2", "gy", "gz"),
    )
    placed = (P(GX, "gy", "gz"), P(GX, "gy", "gz"), P())
    return jax.shard_map(
        shards,
        mesh=torus,
        in_specs=placed,
        out_specs=(P(GX, "gy", "gz"), P(GX, "gy", "gz")),
        check_vma=False,
    )
```

```python
import functools

import jax
import jax.numpy as jnp
from jax import lax
from jax.experimental import pallas as pl
from jax.experimental.pallas import tpu as pltpu
from jax.sharding import Mesh
from jax.sharding import PartitionSpec as P

RINGS = (("gx_1", "gx_2", "gz"), ("gx_0", "gy"))
GX = ("gx_0", "gx_1", "gx_2")
LAP_COEF = (-205.0 / 72.0, 8.0 / 5.0, -1.0 / 5.0, 8.0 / 315.0, -1.0 / 560.0)
STEP = 0.08
F32 = jnp.float32
LANES = 128


def lane_ids(shape):
    return lax.broadcasted_iota(jnp.int32, shape, len(shape) - 1)


def pack(rows_of, count, cells, offset):
    lanes = lane_ids((8, LANES))
    first = last = None
    for q in range(count):
        at = offset + cells * q
        here = (lanes >= at) & (lanes < at + cells)
        rows = rows_of(q)
        head = pltpu.roll(rows, at, 1) if at else rows
        tail = pltpu.roll(rows, (at + cells) % LANES, 1)
        first = jnp.where(here, head, 0.0 if first is None else first)
        last = jnp.where(here, tail, 0.0 if last is None else last)
    return first, last


def unpack(right, left, at, cells):
    lanes = lane_ids((8, LANES))
    high = pltpu.roll(right, (LANES - at) % LANES, 1) if at % LANES else right
    low = pltpu.roll(left, (2 * LANES - cells - at) % LANES, 1)
    return jnp.where(lanes < cells, high, jnp.where(lanes >= LANES - cells, low, 0.0))


def call(body, outs, scratch, *args, scalars=0, flops=0, after=()):
    specs = [pl.BlockSpec(memory_space=pltpu.SMEM)] * scalars
    specs += [pl.BlockSpec(memory_space=pltpu.VMEM)] * (len(args) - scalars)
    specs += [pl.BlockSpec(memory_space=pl.ANY)] * len(after)
    inputs = len(args)
    if after:
        inner = body

        def body(*refs):
            inner(*refs[:inputs], *refs[inputs + len(after) :])

    shapes = [jax.ShapeDtypeStruct(s, F32) for s in outs]
    nbytes = 4 * sum(a.size for a in args) + 4 * sum(s.size for s in shapes)
    return pl.pallas_call(
        body,
        out_shape=shapes,
        in_specs=specs,
        out_specs=[pl.BlockSpec(memory_space=pltpu.VMEM)] * len(outs),
        scratch_shapes=[pltpu.VMEM(s, F32) for s in scratch],
        compiler_params=pltpu.CompilerParams(vmem_limit_bytes=40 * 1024 * 1024),
        cost_estimate=pl.CostEstimate(flops=flops, bytes_accessed=nbytes, transcendentals=0),
    )(*args, *after)


def rows_from(x, q, low, mid, high, edge):
    middle = mid.shape[1] // 8
    if q < edge:
        return low[x, 8 * q : 8 * q + 8, :]
    if q < edge + middle:
        return mid[x, 8 * (q - edge) : 8 * (q - edge) + 8, :]
    return high[x, 8 * (q - edge - middle) : 8 * (q - edge - middle) + 8, :]


def pack_wave(mid, low, high, first, last):
    def plane(x, carry):
        first[x], last[x] = pack(lambda q: rows_from(x, q, low, mid, high, 2), 8, 16, 0)
        return carry

    lax.fori_loop(0, mid.shape[0], plane, 0)


def assemble(own, rim, mid, low, high, right, left):
    own[:, 0:16, :] = low[...]
    own[:, 16:48, :] = mid[...]
    own[:, 48:64, :] = high[...]

    def plane(x, carry):
        for q in range(8):
            rim[x, 8 * q : 8 * q + 8, :] = unpack(right[x], left[x], 16 * q, 16)
        return carry

    lax.fori_loop(0, mid.shape[0], plane, 0)


def halves(x):
    top = x.astype(jnp.bfloat16)
    return top, (x - top.astype(F32)).astype(jnp.bfloat16)


def times(x, matrix_halves):
    top, rest = halves(x)
    big, small = matrix_halves
    dot = functools.partial(jnp.dot, preferred_element_type=F32)
    return dot(top, big) + (dot(top, small) + dot(rest, big))


def slide(src, dst, taps, groups):
    count = dst.shape[0]

    def column(g, carry):
        rows = pl.ds(pl.multiple_of(8 * g, 8), 8)
        sums = {}
        for j in range(count + 16):
            value = src[j, rows, :]
            for a in range(17):
                i = j - a
                if 0 <= i < count:
                    term = taps[a] * value
                    sums[i] = sums[i] + term if a else term
            if j >= 16:
                dst[j - 16, rows, :] = sums.pop(j - 16)
        return carry

    lax.fori_loop(0, groups, column, 0)


def along_rows(src, x, taps, count):
    total = taps[0] * src[x, 0:count, :]
    for b in range(1, 17):
        total = total + taps[b] * src[x, b : b + count, :]
    return total


def smears(
    flags, weights, mid, low, high, right, left, spread, gather, external, corr, potential, outward, inward,
    own, rim, g_own, g_rim, h_own, h_rim, s_own, s_rim, c_own, t_own, t_rim, u_own, u_rim,
):
    assemble(own, rim, mid, low, high, right, left)
    spread_halves = halves(spread[...])
    per = 4

    def along_z(k, carry):
        planes = pl.ds(k * per, per)
        a = own[planes].reshape(per * 64, LANES)
        b = rim[planes].reshape(per * 64, LANES)
        both = jnp.concatenate([a * a, b * b], axis=1)
        out = times(both, spread_halves)
        g_own[planes] = out[:, :LANES].reshape(per, 64, LANES)
        g_rim[planes] = out[:, LANES:].reshape(per, 64, LANES)
        return carry

    lax.fori_loop(0, 48 // per, along_z, 0)
    x_taps = [weights[0, a] for a in range(17)]
    y_taps = [weights[1, a] for a in range(17)]
    slide(g_own, h_own, x_taps, 8)
    slide(g_rim, h_rim, x_taps, 8)

    def source(x, carry):
        for h, e, s in ((h_own, own, s_own), (h_rim, rim, s_rim)):
            coarse = along_rows(h, x, y_taps, 48)
            wave = e[x + 8, 8:56, :]
            density = wave * wave
            s[x] = -1.0 * density * coarse + 0.5 * density * coarse * coarse
            if h is h_own:
                c_own[x] = coarse
        return carry

    lax.fori_loop(0, 32, source, 0)
    slide(s_own, t_own, x_taps[::-1], 6)
    slide(s_rim, t_rim, x_taps[::-1], 6)

    def back(x, carry):
        u_own[x] = along_rows(t_own, x, y_taps[::-1], 32)
        u_rim[x] = along_rows(t_rim, x, y_taps[::-1], 32)
        return carry

    lax.fori_loop(0, 16, back, 0)
    gather_halves = halves(gather[...])
    for k in range(2):
        planes = pl.ds(8 * k, 8)
        both = jnp.concatenate([u_own[planes].reshape(256, LANES), u_rim[planes].reshape(256, LANES)], axis=1)
        smeared = times(both, gather_halves).reshape(8, 32, LANES)
        coarse = c_own[pl.ds(8 + 8 * k, 8), 8:40, :]
        value = -0.5 * coarse * coarse + 0.5 / 3.0 * coarse * coarse * coarse + smeared
        corr[planes] = value
        potential[planes] = value + external[planes]
    upper = flags[0]
    outward[...] = potential[pl.ds(8 * upper, 8)]
    inward[...] = potential[pl.ds(8 * (1 - upper), 8)]


def laplace(own, rim, x, start, count, with_rim):
    lanes = lane_ids((count, LANES))
    rows = slice(start, start + count)
    centers = own[x, rows, :], rim[x, rows, :]
    totals = []
    for ref, other in ((0, 1), (1, 0))[: 2 if with_rim else 1]:
        field = (own, rim)[ref]
        center = centers[ref]
        total = (1.0 + 0.5 * STEP * 3.0 * LAP_COEF[0]) * center
        for k in range(1, 5):
            near = field[x + k, rows, :] + field[x - k, rows, :]
            near = near + (field[x, start + k : start + k + count, :] + field[x, start - k : start - k + count, :])
            ahead = jnp.where(
                lanes < LANES - k, pltpu.roll(center, LANES - k, 1), pltpu.roll(centers[other], LANES - k, 1)
            )
            behind = jnp.where(lanes >= k, pltpu.roll(center, k, 1), pltpu.roll(centers[other], k, 1))
            total = total + (0.5 * STEP * LAP_COEF[k]) * (near + (ahead + behind))
        totals.append(total)
    return totals


def first_step(mid, low, high, right, left, p_own, p_rim, q_own, q_rim, own, rim):
    assemble(own, rim, mid, low, high, right, left)

    def plane(x, carry):
        p_own[x], p_rim[x] = laplace(own, rim, x + 8, 8, 48, True)
        q_own[x] = own[x + 8, 8:56, :]
        q_rim[x] = rim[x + 8, 8:56, :]
        return carry

    lax.fori_loop(0, 32, plane, 0)


def join_planes(flags, mid, outer, inner, joined, head, tail):
    upper = flags[0]
    joined[8:24] = mid[...]

    @pl.when(upper == 0)
    def _():
        joined[0:8] = outer[...]
        joined[24:32] = inner[...]

    @pl.when(upper != 0)
    def _():
        joined[0:8] = inner[...]
        joined[24:32] = outer[...]

    head[...] = joined[:, 0:8, :]
    tail[...] = joined[:, 24:32, :]


def pack_potential(mid, low, high, first, last):
    def plane(x, carry):
        one = pack(lambda q: rows_from(x, q, low, mid, high, 1), 6, 8, 0)
        two = pack(lambda q: rows_from(x + 16, q, low, mid, high, 1), 6, 8, 48)
        first[x] = one[0] + two[0]
        last[x] = one[1] + two[1]
        return carry

    lax.fori_loop(0, 16, plane, 0)


def last_steps(
    flags, p_own, p_rim, q_own, q_rim, mid, low, high, right, left, psi, squares,
    v_own, v_rim, a_own, a_rim, b_own, b_rim,
):
    v_own[:, 0:8, :] = low[...]
    v_own[:, 8:40, :] = mid[...]
    v_own[:, 40:48, :] = high[...]

    def rims(x, carry):
        for q in range(6):
            v_rim[x, 8 * q : 8 * q + 8, :] = unpack(right[x], left[x], 8 * q, 8)
            v_rim[x + 16, 8 * q : 8 * q + 8, :] = unpack(right[x], left[x], 48 + 8 * q, 8)
        return carry

    lax.fori_loop(0, 16, rims, 0)

    def masks(count, edge):
        rows = lax.broadcasted_iota(jnp.int32, (count, LANES), 0) - edge
        lanes = lane_ids((count, LANES))
        in_rows = (rows >= flags[3]) & (rows < flags[4])
        in_rim = ((lanes >= 64) & (flags[5] != 0)) | ((lanes < 64) & (flags[6] != 0))
        rows_one = jnp.where(in_rows, 1.0, 0.0)
        return rows_one, jnp.where(in_rim, rows_one, 0.0)

    def inside(x, edge):
        return jnp.where((x - edge >= flags[1]) & (x - edge < flags[2]), 1.0, 0.0)

    keep_own, keep_rim = masks(48, 8)

    def one(x, carry):
        keep = inside(x, 8)
        a_own[x] = (p_own[x] - STEP * v_own[x] * q_own[x]) * (keep * keep_own)
        a_rim[x] = (p_rim[x] - STEP * v_rim[x] * q_rim[x]) * (keep * keep_rim)
        return carry

    lax.fori_loop(0, 32, one, 0)
    mid_own, mid_rim = masks(40, 4)

    def two(x, carry):
        keep = inside(x, 4)
        own, rim = laplace(a_own, a_rim, x + 4, 4, 40, True)
        v = v_own[x + 4, 4:44, :] * a_own[x + 4, 4:44, :]
        b_own[x] = (own - STEP * v) * (keep * mid_own)
        v = v_rim[x + 4, 4:44, :] * a_rim[x + 4, 4:44, :]
        b_rim[x] = (rim - STEP * v) * (keep * mid_rim)
        return carry

    lax.fori_loop(0, 24, two, 0)

    def three(x, total):
        (own,) = laplace(b_own, b_rim, x + 4, 4, 32, False)
        value = own - STEP * (v_own[x + 8, 8:40, :] * b_own[x + 4, 4:36, :])
        psi[x] = value
        return total + value * value

    total = lax.fori_loop(0, 16, three, jnp.zeros((32, LANES), F32))
    squares[...] = jnp.sum(total, axis=0, keepdims=True)


def band(row, flip):
    places = jnp.arange(256, dtype=jnp.int32)
    places = jnp.where(places < 192, places, places - 256)
    into = places[:LANES] if flip else places
    margin = 0 if flip else 8
    offset = (into[None, :] - places[:, None] if flip else places[:, None] - into[None, :]) + 8
    valid = (into >= -margin) & (into < LANES + margin)
    reach = (places >= -margin - 8) & (places < LANES + margin + 8)
    hits = (offset[:, :, None] == jnp.arange(17, dtype=jnp.int32)) & (valid[None, :] & reach[:, None])[:, :, None]
    return jnp.sum(jnp.where(hits, row, 0.0), axis=2)


def swap_x(outward, inward):
    count = lax.axis_size(GX)
    far = [p for k in range(1, count - 1, 2) for p in ((k, k + 1), (k + 1, k))]
    near = [(k, k ^ 1) for k in range(count)]
    return lax.ppermute(outward, GX, far), lax.ppermute(inward, GX, near)


def shift(head, tail, axis):
    ends = lax.axis_size(axis) - 1
    low = lax.ppermute(tail, axis, [(i, i + 1) for i in range(ends)])
    high = lax.ppermute(head, axis, [(i + 1, i) for i in range(ends)])
    return low, high


def spread_sum(row, groups):
    for axes in groups:
        count = lax.axis_size(axes)
        copies = jnp.broadcast_to(row[None], (count, *row.shape))
        row = jnp.sum(lax.all_to_all(copies, axes, 0, 0, tiled=True), axis=0)
    return jnp.sum(row)


def shards(wave, external, weights):
    at = [lax.axis_index(axis) for axis in (GX, "gy", "gz")]
    last = [at[d] == lax.axis_size(axis) - 1 for d, axis in enumerate((GX, "gy", "gz"))]
    far = 1 << 20
    flags = jnp.stack(
        [
            lax.axis_index("gx_2"),
            jnp.where(at[0] == 0, 0, -far),
            jnp.where(last[0], wave.shape[0], far),
            jnp.where(at[1] == 0, 0, -far),
            jnp.where(last[1], wave.shape[1], far),
            jnp.where(at[2] == 0, 0, 1),
            jnp.where(last[2], 0, 1),
        ]
    ).astype(jnp.int32)
    upper = lax.axis_index("gx_2")
    outer, inner = swap_x(wave, wave)
    mid = jnp.concatenate(
        [jnp.where(upper == 0, outer, inner), wave, jnp.where(upper == 0, inner, outer)], axis=0
    )
    low, high = shift(mid[:, :16, :], mid[:, 16:, :], "gy")
    first, final = call(pack_wave, [(48, 8, LANES)] * 2, [], mid, low, high)
    left, right = shift(first, final, "gz")

    wide, narrow, thin = (48, 64, LANES), (32, 64, LANES), (32, 48, LANES)
    block = wave.shape
    corr, potential, outward, inward = call(
        smears,
        [block, block, (8, 32, LANES), (8, 32, LANES)],
        [wide] * 4 + [narrow] * 2 + [thin] * 3 + [(16, 48, LANES)] * 2 + [block] * 2,
        flags, weights, mid, low, high, right, left, band(weights[2], False), band(weights[2], True), external,
        scalars=2, flops=4 * 10**9,
    )
    v_outer, v_inner = swap_x(outward, inward)
    fields = call(first_step, [thin] * 4, [wide] * 2, mid, low, high, right, left, flops=2 * 10**9)
    v_mid, head, tail = call(
        join_planes,
        [(32, 32, LANES), (32, 8, LANES), (32, 8, LANES)],
        [],
        flags, potential, v_outer, v_inner,
        scalars=1, after=fields[:1],
    )
    v_low, v_high = shift(head, tail, "gy")
    first, final = call(pack_potential, [(16, 8, LANES)] * 2, [], v_mid, v_low, v_high)
    v_left, v_right = shift(first, final, "gz")
    psi, squares = call(
        last_steps,
        [block, (1, LANES)],
        [thin] * 4 + [(24, 40, LANES)] * 2,
        flags, *fields, v_mid, v_low, v_high, v_right, v_left,
        scalars=1, flops=2 * 10**9,
    )
    total = spread_sum(squares, RINGS)
    count = float(psi.size * lax.axis_size(GX) * lax.axis_size("gy") * lax.axis_size("gz"))
    wave_next = psi * lax.rsqrt(total / count + 1e-06)
    return (wave_next, corr)


def solution(mesh):
    torus = Mesh(
        mesh.devices.reshape(4, 2, 2, mesh.shape["gy"], mesh.shape["gz"]),
        ("gx_0", "gx_1", "gx_2", "gy", "gz"),
    )
    placed = (P(GX, "gy", "gz"), P(GX, "gy", "gz"), P())
    return jax.shard_map(
        shards,
        mesh=torus,
        in_specs=placed,
        out_specs=(P(GX, "gy", "gz"), P(GX, "gy", "gz")),
        check_vma=False,
    )
```

```python
import functools

import jax
import jax.numpy as jnp
from jax import lax
from jax.experimental import pallas as pl
from jax.experimental.pallas import tpu as pltpu
from jax.sharding import Mesh
from jax.sharding import PartitionSpec as P

RINGS = (("gx_1", "gx_2", "gz"), ("gx_0", "gy"))
GX = ("gx_0", "gx_1", "gx_2")
LAP_COEF = (-205.0 / 72.0, 8.0 / 5.0, -1.0 / 5.0, 8.0 / 315.0, -1.0 / 560.0)
STEP = 0.08
F32 = jnp.float32
LANES = 128


def lane_ids(shape):
    return lax.broadcasted_iota(jnp.int32, shape, len(shape) - 1)


def pack(rows_of, count, cells, offset):
    lanes = lane_ids((8, LANES))
    first = last = None
    for q in range(count):
        at = offset + cells * q
        here = (lanes >= at) & (lanes < at + cells)
        rows = rows_of(q)
        head = pltpu.roll(rows, at, 1) if at else rows
        tail = pltpu.roll(rows, (at + cells) % LANES, 1)
        first = jnp.where(here, head, 0.0 if first is None else first)
        last = jnp.where(here, tail, 0.0 if last is None else last)
    return first, last


def unpack(right, left, at, cells):
    lanes = lane_ids((8, LANES))
    high = pltpu.roll(right, (LANES - at) % LANES, 1) if at % LANES else right
    low = pltpu.roll(left, (2 * LANES - cells - at) % LANES, 1)
    return jnp.where(lanes < cells, high, jnp.where(lanes >= LANES - cells, low, 0.0))


def skipping(body, start, count, *refs):
    body(*refs[:start], *refs[start + count :])


def call(body, outs, scratch, *args, scalars=0, flops=0, aliases=None, after=()):
    specs = [pl.BlockSpec(memory_space=pltpu.SMEM)] * scalars
    specs += [pl.BlockSpec(memory_space=pltpu.VMEM)] * (len(args) - scalars)
    specs += [pl.BlockSpec(memory_space=pl.ANY)] * len(after)
    body = functools.partial(skipping, body, len(args), len(after))
    shapes = [jax.ShapeDtypeStruct(s, F32) for s in outs]
    nbytes = 4 * sum(a.size for a in args) + 4 * sum(s.size for s in shapes)
    return pl.pallas_call(
        body,
        out_shape=shapes,
        in_specs=specs,
        out_specs=[pl.BlockSpec(memory_space=pltpu.VMEM)] * len(outs),
        scratch_shapes=[pltpu.VMEM(s, F32) for s in scratch],
        input_output_aliases=aliases or {},
        compiler_params=pltpu.CompilerParams(vmem_limit_bytes=20 * 1024 * 1024),
        cost_estimate=pl.CostEstimate(flops=flops, bytes_accessed=nbytes, transcendentals=0),
    )(*args, *after)


def cut(wave, external, head, tail):
    head[:, 0:24, :] = wave[:, 0:24, :]
    head[:, 24:32, :] = external[:, 0:8, :]
    tail[:, 0:24, :] = wave[:, 8:32, :]
    tail[:, 24:32, :] = external[:, 24:32, :]


def cut_outer(outer, head, tail):
    head[...] = outer[:, 0:24, :]
    tail[...] = outer[:, 8:32, :]


def stacked(x, low, mid, high):
    def rows_of(q):
        for ref, start, stop in (low, mid, high):
            count = (stop - start) // 8
            if q < count:
                return ref[x, start + 8 * q : start + 8 * q + 8, :]
            q -= count

    return rows_of


def pack_wave(wave, low, high, first, last):
    def plane(x, carry):
        rows_of = stacked(x, (low, 0, 24), (wave, 0, 32), (high, 0, 24))
        for r in range(2):
            rows = slice(8 * r, 8 * r + 8)
            first[x, rows, :], last[x, rows, :] = pack(lambda q: rows_of(q + 5 * r), 5, 24, 0)
        return carry

    lax.fori_loop(0, 16, plane, 0)


def pack_both(wave, external, low, high, first, last):
    pack_wave(wave, low, high, first, last)

    def plane(x, carry):
        rows_of = stacked(x, (low, 24, 32), (external, 0, 32), (high, 24, 32))
        first[x, 16:24, :], last[x, 16:24, :] = pack(rows_of, 6, 8, 0)
        return carry

    lax.fori_loop(0, 16, plane, 0)


def fill(own, rim, base, mid, low, high, right, left):
    def plane(x, carry):
        own[base + x, 0:24, :] = low[x, 0:24, :]
        own[base + x, 24:56, :] = mid[x]
        own[base + x, 56:80, :] = high[x, 0:24, :]
        for g in range(10):
            rows = slice(8 * (g // 5), 8 * (g // 5) + 8)
            rim[base + x, 8 * g : 8 * g + 8, :] = unpack(right[x, rows, :], left[x, rows, :], 24 * (g % 5), 24)
        return carry

    lax.fori_loop(0, 16, plane, 0)


def halves(x):
    top = x.astype(jnp.bfloat16)
    return top, (x - top.astype(F32)).astype(jnp.bfloat16)


def times(x, matrix_halves):
    top, rest = halves(x)
    big, small = matrix_halves
    dot = functools.partial(jnp.dot, preferred_element_type=F32)
    return dot(top, big) + (dot(top, small) + dot(rest, big))


def slide(src, dst, taps, groups):
    count = dst.shape[0]

    def column(g, carry):
        rows = pl.ds(pl.multiple_of(8 * g, 8), 8)
        sums = {}
        for j in range(count + 16):
            value = src[j, rows, :]
            for a in range(17):
                i = j - a
                if 0 <= i < count:
                    term = taps[a] * value
                    sums[i] = sums[i] + term if a else term
            if j >= 16:
                dst[j - 16, rows, :] = sums.pop(j - 16)
        return carry

    lax.fori_loop(0, groups, column, 0)


def along_rows(src, x, taps, count):
    total = taps[0] * src[x, 0:count, :]
    for b in range(1, 17):
        total = total + taps[b] * src[x, b : b + count, :]
    return total


def along_z(own, rim, g_own, g_rim, base, spread_halves):
    def chunk(k, carry):
        planes = pl.ds(base + 2 * k, 2)
        a = own[planes].reshape(160, LANES)
        b = rim[planes].reshape(160, LANES)
        out = times(jnp.concatenate([a * a, b * b], axis=1), spread_halves)
        g_own[planes] = out[:, :LANES].reshape(2, 80, LANES)
        g_rim[planes] = out[:, LANES:].reshape(2, 80, LANES)
        return carry

    lax.fori_loop(0, 8, chunk, 0)


def prepare(
    flags, spread, wave, low, high, right, left, inner, i_low, i_high, i_right, i_left, own, rim, g_own, g_rim
):
    spread_halves = halves(spread[...])
    base = 32 * (1 - flags[0])
    fill(own, rim, 16, wave, low, high, right, left)
    along_z(own, rim, g_own, g_rim, 16, spread_halves)
    fill(own, rim, base, inner, i_low, i_high, i_right, i_left)
    along_z(own, rim, g_own, g_rim, base, spread_halves)


def smears(
    flags, weights, spread, gather, external, low, high, right, left, outer, o_low, o_high, o_right, o_left,
    own_in, rim_in, g_own_in, g_rim_in, corr, v_own, v_rim, outward, inward, own, rim, g_own, g_rim,
    h_own, h_rim, s_own, s_rim, c_own, c_rim, t_own, t_rim, u_own, u_rim,
):
    upper = flags[0]
    base = 32 * upper
    fill(own, rim, base, outer, o_low, o_high, o_right, o_left)
    along_z(own, rim, g_own, g_rim, base, halves(spread[...]))
    x_taps = [weights[0, a] for a in range(17)]
    y_taps = [weights[1, a] for a in range(17)]
    slide(g_own, h_own, x_taps, 10)
    slide(g_rim, h_rim, x_taps, 10)

    def source(x, carry):
        for h, e, s, c in ((h_own, own, s_own, c_own), (h_rim, rim, s_rim, c_rim)):
            coarse = along_rows(h, x, y_taps, 64)
            wave = e[x + 8, 8:72, :]
            density = wave * wave
            s[x] = -1.0 * density * coarse + 0.5 * density * coarse * coarse
            c[x] = coarse
        return carry

    lax.fori_loop(0, 32, source, 0)
    slide(s_own, t_own, x_taps[::-1], 8)
    slide(s_rim, t_rim, x_taps[::-1], 8)

    def back(x, carry):
        u_own[x] = along_rows(t_own, x, y_taps[::-1], 48)
        u_rim[x] = along_rows(t_rim, x, y_taps[::-1], 48)
        return carry

    lax.fori_loop(0, 16, back, 0)
    gather_halves = halves(gather[...])

    def finish(k, carry):
        planes = pl.ds(4 * k, 4)
        both = jnp.concatenate([u_own[planes].reshape(192, LANES), u_rim[planes].reshape(192, LANES)], axis=1)
        smeared = times(both, gather_halves)
        for c, v, part in ((c_own, v_own, smeared[:, :LANES]), (c_rim, v_rim, smeared[:, LANES:])):
            coarse = c[pl.ds(8 + 4 * k, 4), 8:56, :]
            v[planes] = -0.5 * coarse * coarse + 0.5 / 3.0 * coarse * coarse * coarse + part.reshape(4, 48, LANES)
        corr[planes] = v_own[planes, 8:40, :]
        v_own[planes, 0:8, :] += low[planes, 24:32, :]
        v_own[planes, 8:40, :] += external[planes]
        v_own[planes, 40:48, :] += high[planes, 24:32, :]
        for i in range(4):
            x = 4 * k + i
            for q in range(6):
                v_rim[x, 8 * q : 8 * q + 8, :] += unpack(right[x, 16:24, :], left[x, 16:24, :], 8 * q, 8)
        return carry

    lax.fori_loop(0, 4, finish, 0)

    lanes = lane_ids((8, LANES))
    for out, side in ((outward, upper), (inward, 1 - upper)):
        edge, beyond = 12 * side, 4 + 4 * side
        rims = jnp.zeros((8, LANES), F32)
        for i in range(4):
            for q in range(5):
                out[5 * i + q] = v_own[edge + i, 4 + 8 * q : 12 + 8 * q, :]
            for q in range(4):
                out[20 + 4 * i + q] = v_own[beyond + i, 8 + 8 * q : 16 + 8 * q, :]
                at = 8 * (4 * i + q)
                here = (lanes >= at) & (lanes < at + 8)
                rims = jnp.where(here, pltpu.roll(v_rim[edge + i, 8 + 8 * q : 16 + 8 * q, :], (at + 4) % LANES, 1), rims)
        out[36] = rims


def laplace(own, rim, x, start, count, with_rim):
    lanes = lane_ids((count, LANES))
    rows = slice(start, start + count)
    centers = own[x, rows, :], rim[x, rows, :]
    totals = []
    for ref, other in ((0, 1), (1, 0))[: 2 if with_rim else 1]:
        field = (own, rim)[ref]
        center = centers[ref]
        total = (1.0 + 0.5 * STEP * 3.0 * LAP_COEF[0]) * center
        for k in range(1, 5):
            near = field[x + k, rows, :] + field[x - k, rows, :]
            near = near + (field[x, start + k : start + k + count, :] + field[x, start - k : start - k + count, :])
            ahead = jnp.where(
                lanes < LANES - k, pltpu.roll(center, LANES - k, 1), pltpu.roll(centers[other], LANES - k, 1)
            )
            behind = jnp.where(lanes >= k, pltpu.roll(center, k, 1), pltpu.roll(centers[other], k, 1))
            total = total + (0.5 * STEP * LAP_COEF[k]) * (near + (ahead + behind))
        totals.append(total)
    return totals


def first_step(own, rim, p_own, p_rim):
    def plane(x, carry):
        p_own[x], p_rim[x] = laplace(own, rim, x + 8, 16, 48, True)
        return carry

    lax.fori_loop(0, 32, plane, 0)


def last_steps(
    flags, p_own, p_rim, q_own, q_rim, mid_own, mid_rim, outer, inner, psi, squares,
    v_own, v_rim, a_own, a_rim, b_own, b_rim,
):
    upper = flags[0]
    v_own[8:24] = mid_own[...]
    v_rim[8:24] = mid_rim[...]
    lanes = lane_ids((8, LANES))
    for ref, side in ((outer, upper), (inner, 1 - upper)):
        edge, beyond = 4 + 20 * side, 28 * side
        for i in range(4):
            v_own[beyond + i] = jnp.zeros((48, LANES), F32)
            v_rim[beyond + i] = jnp.zeros((48, LANES), F32)
            v_own[edge + i] = jnp.zeros((48, LANES), F32)
            v_rim[edge + i] = jnp.zeros((48, LANES), F32)
            for q in range(5):
                v_own[edge + i, 4 + 8 * q : 12 + 8 * q, :] = ref[5 * i + q]
            for q in range(4):
                v_own[beyond + i, 8 + 8 * q : 16 + 8 * q, :] = ref[20 + 4 * i + q]
                rim = pltpu.roll(ref[36], LANES - 4 - 8 * (4 * i + q) + (LANES if 4 * i + q == 15 else 0), 1)
                v_rim[edge + i, 8 + 8 * q : 16 + 8 * q, :] = jnp.where((lanes < 4) | (lanes >= LANES - 4), rim, 0.0)

    def masks(count, edge):
        rows = lax.broadcasted_iota(jnp.int32, (count, LANES), 0) - edge
        lanes = lane_ids((count, LANES))
        in_rows = (rows >= flags[3]) & (rows < flags[4])
        in_rim = ((lanes >= 64) & (flags[5] != 0)) | ((lanes < 64) & (flags[6] != 0))
        rows_one = jnp.where(in_rows, 1.0, 0.0)
        return rows_one, jnp.where(in_rim, rows_one, 0.0)

    def inside(x, edge):
        return jnp.where((x - edge >= flags[1]) & (x - edge < flags[2]), 1.0, 0.0)

    keep_own, keep_rim = masks(48, 8)

    def one(x, carry):
        keep = inside(x, 8)
        a_own[x] = (p_own[x] - STEP * v_own[x] * q_own[x + 8, 16:64, :]) * (keep * keep_own)
        a_rim[x] = (p_rim[x] - STEP * v_rim[x] * q_rim[x + 8, 16:64, :]) * (keep * keep_rim)
        return carry

    lax.fori_loop(0, 32, one, 0)
    mid_own, mid_rim = masks(40, 4)

    def two(x, carry):
        keep = inside(x, 4)
        own, rim = laplace(a_own, a_rim, x + 4, 4, 40, True)
        v = v_own[x + 4, 4:44, :] * a_own[x + 4, 4:44, :]
        b_own[x] = (own - STEP * v) * (keep * mid_own)
        v = v_rim[x + 4, 4:44, :] * a_rim[x + 4, 4:44, :]
        b_rim[x] = (rim - STEP * v) * (keep * mid_rim)
        return carry

    lax.fori_loop(0, 24, two, 0)

    def three(x, total):
        (own,) = laplace(b_own, b_rim, x + 4, 4, 32, False)
        value = own - STEP * (v_own[x + 8, 8:40, :] * b_own[x + 4, 4:36, :])
        psi[x] = value
        return total + value * value

    total = lax.fori_loop(0, 16, three, jnp.zeros((32, LANES), F32))
    squares[...] = jnp.sum(total, axis=0, keepdims=True)


def scale(count, rows, psi, out):
    total = jnp.sum(rows[...].reshape(-1, LANES), axis=0, keepdims=True)
    total = jnp.sum(total, axis=1, keepdims=True)
    factor = lax.rsqrt(total / count + 1e-06)
    out[...] = psi[...] * factor[None]


def band(row, flip):
    places = jnp.arange(256, dtype=jnp.int32)
    places = jnp.where(places < 192, places, places - 256)
    margin = 8 if flip else 16
    offset = (places[None, :] - places[:, None] if flip else places[:, None] - places[None, :]) + 8
    valid = (places >= -margin) & (places < LANES + margin)
    reach = (places >= -margin - 8) & (places < LANES + margin + 8)
    hits = (offset[:, :, None] == jnp.arange(17, dtype=jnp.int32)) & (valid[None, :] & reach[:, None])[:, :, None]
    return jnp.sum(jnp.where(hits, row, 0.0), axis=2)


def swap_far(planes):
    count = lax.axis_size(GX)
    return lax.ppermute(planes, GX, [p for k in range(1, count - 1, 2) for p in ((k, k + 1), (k + 1, k))])


def swap_near(planes):
    return lax.ppermute(planes, GX, [(k, k ^ 1) for k in range(lax.axis_size(GX))])


def shift(head, tail, axis):
    ends = lax.axis_size(axis) - 1
    low = lax.ppermute(tail, axis, [(i, i + 1) for i in range(ends)])
    high = lax.ppermute(head, axis, [(i + 1, i) for i in range(ends)])
    return low, high


def spread(row, axes):
    count = lax.axis_size(axes)
    return lax.all_to_all(jnp.broadcast_to(row[None], (count, *row.shape)), axes, 0, 0, tiled=True)


def shards(wave, external, weights):
    at = [lax.axis_index(axis) for axis in (GX, "gy", "gz")]
    last = [at[d] == lax.axis_size(axis) - 1 for d, axis in enumerate((GX, "gy", "gz"))]
    far = 1 << 20
    flags = jnp.stack(
        [
            lax.axis_index("gx_2"),
            jnp.where(at[0] == 0, 0, -far),
            jnp.where(last[0], wave.shape[0], far),
            jnp.where(at[1] == 0, 0, -far),
            jnp.where(last[1], wave.shape[1], far),
            jnp.where(at[2] == 0, 0, 1),
            jnp.where(last[2], 0, 1),
        ]
    ).astype(jnp.int32)
    block = wave.shape
    outer, inner = swap_far(wave), swap_near(wave)
    low, high = shift(*call(cut, [block] * 2, [], wave, external), "gy")
    first, final = call(pack_both, [(16, 24, LANES)] * 2, [], wave, external, low, high)
    left, right = shift(first, final, "gz")
    i_low, i_high, i_left, i_right = (swap_near(a) for a in (low, high, left, right))
    o_low, o_high = shift(*call(cut_outer, [(16, 24, LANES)] * 2, [], outer, after=(left, right, i_low, i_high)), "gy")
    first, final = call(pack_wave, [(16, 16, LANES)] * 2, [], outer, o_low, o_high)
    o_left, o_right = shift(first, final, "gz")

    wide, thin, box = (48, 80, LANES), (32, 48, LANES), (16, 48, LANES)
    smear_z, gather_z = band(weights[2], False), band(weights[2], True)
    fields = call(
        prepare, [wide] * 4, [],
        flags, smear_z, wave, low, high, right, left, inner, i_low, i_high, i_right, i_left,
        scalars=1, flops=2 * 10**9,
    )
    corr, v_own, v_rim, outward, inward, own, rim, _, _ = call(
        smears,
        [block, box, box, (37, 8, LANES), (37, 8, LANES)] + [wide] * 4,
        [(32, 80, LANES)] * 2 + [(32, 64, LANES)] * 4 + [(16, 64, LANES)] * 2 + [box] * 2,
        flags, weights, smear_z, gather_z, external, low, high, right, left,
        outer, o_low, o_high, o_right, o_left, *fields,
        scalars=2, flops=4 * 10**9, aliases={14: 5, 15: 6, 16: 7, 17: 8},
    )
    v_outer, v_inner = swap_far(outward), swap_near(inward)
    p_own, p_rim = call(first_step, [thin] * 2, [], own, rim, flops=2 * 10**9)
    psi, squares = call(
        last_steps,
        [block, (1, LANES)],
        [thin] * 4 + [(24, 40, LANES)] * 2,
        flags, p_own, p_rim, own, rim, v_own, v_rim, v_outer, v_inner,
        scalars=1, flops=2 * 10**9,
    )
    rows = spread(jnp.sum(spread(squares, RINGS[0]), axis=0), RINGS[1])
    count = float(psi.size * lax.axis_size(GX) * lax.axis_size("gy") * lax.axis_size("gz"))
    (wave_next,) = call(functools.partial(scale, count), [block], [], rows, psi)
    return (wave_next, corr)


def solution(mesh):
    torus = Mesh(
        mesh.devices.reshape(4, 2, 2, mesh.shape["gy"], mesh.shape["gz"]),
        ("gx_0", "gx_1", "gx_2", "gy", "gz"),
    )
    placed = (P(GX, "gy", "gz"), P(GX, "gy", "gz"), P())
    return jax.shard_map(
        shards,
        mesh=torus,
        in_specs=placed,
        out_specs=(P(GX, "gy", "gz"), P(GX, "gy", "gz")),
        check_vma=False,
    )
```

```python
import functools

import jax
import jax.numpy as jnp
import numpy as np
from jax import lax
from jax.experimental import pallas as pl
from jax.experimental.pallas import tpu as pltpu
from jax.sharding import Mesh
from jax.sharding import PartitionSpec as P

RINGS = (("gx_1", "gx_2", "gz"), ("gx_0", "gy"))
GX = ("gx_0", "gx_1", "gx_2")
LAP_COEF = (-205.0 / 72.0, 8.0 / 5.0, -1.0 / 5.0, 8.0 / 315.0, -1.0 / 560.0)
STEP = 0.08
F32 = jnp.float32
LANES = 128


def lane_ids(shape):
    return lax.broadcasted_iota(jnp.int32, shape, len(shape) - 1)


def pack(rows_of, count, cells, offset):
    lanes = lane_ids((8, LANES))
    first = last = None
    for q in range(count):
        at = offset + cells * q
        here = (lanes >= at) & (lanes < at + cells)
        rows = rows_of(q)
        head = pltpu.roll(rows, at, 1) if at else rows
        tail = pltpu.roll(rows, (at + cells) % LANES, 1)
        first = jnp.where(here, head, 0.0 if first is None else first)
        last = jnp.where(here, tail, 0.0 if last is None else last)
    return first, last


def unpack(right, left, at, cells):
    lanes = lane_ids((8, LANES))
    high = pltpu.roll(right, (LANES - at) % LANES, 1) if at % LANES else right
    low = pltpu.roll(left, (2 * LANES - cells - at) % LANES, 1)
    return jnp.where(lanes < cells, high, jnp.where(lanes >= LANES - cells, low, 0.0))


def skipping(body, start, count, *refs):
    body(*refs[:start], *refs[start + count :])


def call(body, outs, scratch, *args, scalars=0, flops=1000, after=()):
    specs = [pl.BlockSpec(memory_space=pltpu.SMEM)] * scalars
    specs += [pl.BlockSpec(memory_space=pltpu.VMEM)] * (len(args) - scalars)
    specs += [pl.BlockSpec(memory_space=pl.ANY)] * len(after)
    body = functools.partial(skipping, body, len(args), len(after))
    shapes = [jax.ShapeDtypeStruct(s, F32) for s in outs]
    nbytes = 4 * sum(a.size for a in args) + 4 * sum(s.size for s in shapes)
    return pl.pallas_call(
        body,
        out_shape=shapes,
        in_specs=specs,
        out_specs=[pl.BlockSpec(memory_space=pltpu.VMEM)] * len(outs),
        scratch_shapes=[pltpu.VMEM(s, F32) for s in scratch],
        compiler_params=pltpu.CompilerParams(vmem_limit_bytes=20 * 1024 * 1024),
        cost_estimate=pl.CostEstimate(flops=flops, bytes_accessed=nbytes, transcendentals=0),
    )(*args, *after)


def cut(wave, external, head, tail):
    head[:, 0:24, :] = wave[:, 0:24, :]
    head[:, 24:32, :] = external[:, 0:8, :]
    tail[:, 0:24, :] = wave[:, 8:32, :]
    tail[:, 24:32, :] = external[:, 24:32, :]


def cut_outer(outer, head, tail):
    head[...] = outer[:, 0:24, :]
    tail[...] = outer[:, 8:32, :]


def stacked(x, low, mid, high):
    def rows_of(q):
        for ref, start, stop in (low, mid, high):
            count = (stop - start) // 8
            if q < count:
                return ref[x, start + 8 * q : start + 8 * q + 8, :]
            q -= count

    return rows_of


def pack_cells(wave, low, high, first, last):
    def plane(x, carry):
        rows_of = stacked(x, (low, 0, 24), (wave, 0, 32), (high, 0, 24))
        for r in range(2):
            rows = slice(8 * r, 8 * r + 8)
            first[x, rows, :], last[x, rows, :] = pack(lambda q: rows_of(q + 5 * r), 5, 24, 0)
        return carry

    lax.fori_loop(0, 16, plane, 0, unroll=2)


def pack_both(wave, external, low, high, first, last, rows):
    pack_cells(wave, low, high, first, last)
    rows[:, 0:24, :] = low[:, 0:24, :]
    rows[:, 24:48, :] = high[:, 0:24, :]

    def plane(x, carry):
        rows_of = stacked(x, (low, 24, 32), (external, 0, 32), (high, 24, 32))
        first[x, 16:24, :], last[x, 16:24, :] = pack(rows_of, 6, 8, 0)
        return carry

    lax.fori_loop(0, 16, plane, 0, unroll=2)


def pack_outer(wave, low, high, right, left, first, last, sides):
    pack_cells(wave, low, high, first, last)
    sides[:, 0:16, :] = right[:, 0:16, :]
    sides[:, 16:32, :] = left[:, 0:16, :]


def fill(own, rim, base, mid, low, high, right, left):
    def plane(x, carry):
        own[base + x, 0:24, :] = low[x, 0:24, :]
        own[base + x, 24:56, :] = mid[x]
        own[base + x, 56:80, :] = high[x, 0:24, :]
        for g in range(10):
            rows = slice(8 * (g // 5), 8 * (g // 5) + 8)
            rim[base + x, 8 * g : 8 * g + 8, :] = unpack(right[x, rows, :], left[x, rows, :], 24 * (g % 5), 24)
        return carry

    lax.fori_loop(0, 16, plane, 0, unroll=4)


def halves(x):
    top = x.astype(jnp.bfloat16)
    return top, (x - top.astype(F32)).astype(jnp.bfloat16)


def times(x, matrix_halves):
    top, rest = halves(x)
    big, small = matrix_halves
    dot = functools.partial(jnp.dot, preferred_element_type=F32)
    return dot(top, big) + (dot(top, small) + dot(rest, big))


def slide(src, base, dst, taps, groups):
    count = dst.shape[0]

    def column(g, carry):
        rows = pl.ds(pl.multiple_of(8 * g, 8), 8)
        sums = {}
        for j in range(count + 16):
            value = src[base + j, rows, :]
            for a in range(17):
                i = j - a
                if 0 <= i < count:
                    term = taps[a] * value
                    sums[i] = sums[i] + term if a else term
            if j >= 16:
                dst[j - 16, rows, :] = sums.pop(j - 16)
        return carry

    lax.fori_loop(0, groups, column, 0)


def along_rows(src, x, taps, count):
    total = taps[0] * src[x, 0:count, :]
    for b in range(1, 17):
        total = total + taps[b] * src[x, b : b + count, :]
    return total


def along_z(own, rim, g_own, g_rim, base, spread_halves, start=None):
    start = base if start is None else start

    def chunk(k, carry):
        planes = pl.ds(start + 8 * k, 8)
        a = own[planes].reshape(640, LANES)
        b = rim[planes].reshape(640, LANES)
        out = times(jnp.concatenate([a * a, b * b], axis=1), spread_halves)
        planes = pl.ds(base + 8 * k, 8)
        g_own[planes] = out[:, :LANES].reshape(8, 80, LANES)
        g_rim[planes] = out[:, LANES:].reshape(8, 80, LANES)
        return carry

    lax.fori_loop(0, 2, chunk, 0)


def sources(weights, field, at, g_own, g_rim, base, s_own, s_rim, to, c_own, c_rim, h_own, h_rim):
    x_taps = [weights[0, a] for a in range(17)]
    y_taps = [weights[1, a] for a in range(17)]
    slide(g_own, base, h_own, x_taps, 10)
    slide(g_rim, base, h_rim, x_taps, 10)

    def source(x, carry):
        for h, e, s, c in ((h_own, field[0], s_own, c_own), (h_rim, field[1], s_rim, c_rim)):
            coarse = along_rows(h, x, y_taps, 64)
            wave = e[at + x, 8:72, :]
            density = wave * wave
            s[to + x] = -1.0 * density * coarse + 0.5 * density * coarse * coarse
            c[x] = coarse
        return carry

    lax.fori_loop(0, 16, source, 0)


def band(weights, flip):
    def places(dim):
        at = lax.broadcasted_iota(jnp.int32, (256, 256), dim)
        return jnp.where(at < 192, at, at - 256)

    start, end = places(0), places(1)
    margin = 8 if flip else 16
    offset = (end - start if flip else start - end) + 8
    used = (end >= -margin) & (end < LANES + margin) & (start >= -margin - 8) & (start < LANES + margin + 8)
    offset = jnp.where(used, offset, -1)
    matrix = jnp.zeros((256, 256), F32)
    for tap in range(17):
        matrix = jnp.where(offset == tap, weights[2, tap], matrix)
    return matrix


def bands(weights, spread, gather):
    spread[...] = band(weights, False)
    gather[...] = band(weights, True)


def prepare(
    flags, weights, spread, wave, low, high, right, left, inner, i_rows, i_sides,
    own, rim, g_own, g_rim, s_own, s_rim, c_own, c_rim, k_own, k_rim, h_own, h_rim,
):
    spread_halves = halves(spread[...])
    upper = flags[0]
    mine, other = 16 * upper, 16 * (1 - upper)
    fill(own, rim, mine, wave, low, high, right, left)
    i_low, i_high = i_rows.at[:, 0:24, :], i_rows.at[:, 24:48, :]
    i_right, i_left = i_sides.at[:, 0:16, :], i_sides.at[:, 16:32, :]
    fill(own, rim, other, inner, i_low, i_high, i_right, i_left)
    along_z(own, rim, k_own, k_rim, 0, spread_halves)
    along_z(own, rim, k_own, k_rim, 16, spread_halves)
    g_own[...] = k_own[pl.ds(mine, 16)]
    g_rim[...] = k_rim[pl.ds(mine, 16)]
    sources(weights, (own, rim), 8, k_own, k_rim, 0, s_own, s_rim, 0, c_own, c_rim, h_own, h_rim)


def potentials(
    side, weights, gather, external, low, high, right, left, s_own, s_rim, c_own, c_rim, at_c,
    corr, v_own, v_rim, slab, t_own, t_rim, u_own, u_rim,
):
    x_taps = [weights[0, 16 - a] for a in range(17)]
    y_taps = [weights[1, 16 - a] for a in range(17)]
    base = 8 * side
    slide(s_own, base, t_own, x_taps, 8)
    slide(s_rim, base, t_rim, x_taps, 8)

    def back(x, carry):
        u_own[x] = along_rows(t_own, x, y_taps, 48)
        u_rim[x] = along_rows(t_rim, x, y_taps, 48)
        return carry

    lax.fori_loop(0, 8, back, 0)
    both = jnp.concatenate([u_own[...].reshape(384, LANES), u_rim[...].reshape(384, LANES)], axis=1)
    smeared = times(both, halves(gather[...]))
    planes = pl.ds(base, 8)
    for c, v, part in ((c_own, v_own, smeared[:, :LANES]), (c_rim, v_rim, smeared[:, LANES:])):
        coarse = c[pl.ds(at_c, 8), 8:56, :]
        v[...] = -0.5 * coarse * coarse + 0.5 / 3.0 * coarse * coarse * coarse + part.reshape(8, 48, LANES)
    corr[...] = v_own[:, 8:40, :]
    v_own[:, 0:8, :] += low[planes, 24:32, :]
    v_own[:, 8:40, :] += external[planes]
    v_own[:, 40:48, :] += high[planes, 24:32, :]
    for x in range(8):
        for q in range(6):
            v_rim[x, 8 * q : 8 * q + 8, :] += unpack(right[base + x, 16:24, :], left[base + x, 16:24, :], 8 * q, 8)

    lanes = lane_ids((8, LANES))
    edge, beyond = 4 * side, 4 - 4 * side
    rims = jnp.zeros((8, LANES), F32)
    for i in range(4):
        for q in range(5):
            slab[5 * i + q] = v_own[edge + i, 4 + 8 * q : 12 + 8 * q, :]
        for q in range(4):
            slab[20 + 4 * i + q] = v_own[beyond + i, 8 + 8 * q : 16 + 8 * q, :]
            at = 8 * (4 * i + q)
            these = (lanes >= at) & (lanes < at + 8)
            rims = jnp.where(these, pltpu.roll(v_rim[edge + i, 8 + 8 * q : 16 + 8 * q, :], (at + 4) % LANES, 1), rims)
    slab[36] = rims


def far_side(
    flags, weights, spread, gather, external, low, high, right, left, outer, o_low, o_high, o_right, o_left,
    own, rim, g_own, g_rim, s_own, s_rim, out_own, out_rim, s_all_own, s_all_rim, corr, v_own, v_rim, slab,
    e_own, e_rim, k_own, k_rim, c_own, c_rim, h_own, h_rim, t_own, t_rim, u_own, u_rim,
):
    upper = flags[0]
    below = 1 - upper
    fill(out_own, out_rim, 0, outer, o_low, o_high, o_right, o_left)
    along_z(out_own, out_rim, k_own, k_rim, 16 * upper, halves(spread[...]), 0)
    mine = pl.ds(16 * below, 16)
    k_own[mine] = g_own[...]
    k_rim[mine] = g_rim[...]
    for e, out, field in ((e_own, out_own, own), (e_rim, out_rim, rim)):
        e[pl.ds(8 * upper, 8)] = out[pl.ds(8 * below, 8)]
        e[pl.ds(8 * below, 8)] = field[pl.ds(24 * upper, 8)]
    for s_all, s in ((s_all_own, s_own), (s_all_rim, s_rim)):
        s_all[pl.ds(16 * below, 16)] = s[...]
    sources(
        weights, (e_own, e_rim), 0, k_own, k_rim, 0, s_all_own, s_all_rim, 16 * upper, c_own, c_rim, h_own, h_rim
    )
    potentials(
        upper, weights, gather, external, low, high, right, left, s_all_own, s_all_rim, c_own, c_rim, 8 * below,
        corr, v_own, v_rim, slab, t_own, t_rim, u_own, u_rim,
    )


def near_side(
    flags, weights, gather, external, low, high, right, left, s_own, s_rim, c_own, c_rim, far_corr,
    corr, v_own, v_rim, slab, near_corr, t_own, t_rim, u_own, u_rim,
):
    upper = flags[0]
    below = 1 - upper
    potentials(
        below, weights, gather, external, low, high, right, left, s_own, s_rim, c_own, c_rim, 8 * upper,
        near_corr, v_own, v_rim, slab, t_own, t_rim, u_own, u_rim,
    )
    corr[pl.ds(8 * below, 8)] = near_corr[...]
    corr[pl.ds(8 * upper, 8)] = far_corr[...]


def laplace(own, rim, x, count, start, rows, shifts, with_rim):
    planes = pl.ds(x, count)
    here = slice(start, start + rows)
    centers = own[planes, here, :], rim[planes, here, :]
    flat = [c.reshape(count * rows, LANES) for c in centers]
    shifted = times(jnp.concatenate(flat, axis=1), shifts)
    answers = []
    for ref in range(2 if with_rim else 1):
        field = (own, rim)[ref]
        part = shifted[:, LANES * ref : LANES * ref + LANES].reshape(count, rows, LANES)
        total = (1.0 + 0.5 * STEP * 3.0 * LAP_COEF[0]) * centers[ref] + part
        for k in range(1, 5):
            near = field[pl.ds(x + k, count), here, :] + field[pl.ds(x - k, count), here, :]
            near = near + (field[planes, start + k : start + k + rows, :] + field[planes, start - k : start - k + rows, :])
            total = total + (0.5 * STEP * LAP_COEF[k]) * near
        answers.append(total)
    return answers


def ring_shifts():
    gap = np.abs(np.arange(256)[:, None] - np.arange(256)[None, :])
    gap = np.minimum(gap, 256 - gap)
    matrix = np.zeros((256, 256), np.float32)
    for k in range(1, 5):
        matrix[gap == k] = 0.5 * STEP * LAP_COEF[k]
    return matrix


def first_step(flags, shifts, own, rim, out_own, out_rim, p_own, p_rim, e_own, e_rim):
    shift_halves = halves(shifts[...])
    upper = flags[0]
    for e, field, out in ((e_own, own, out_own), (e_rim, rim, out_rim)):
        e[pl.ds(16 * (1 - upper), 32)] = field[...]
        e[pl.ds(32 * upper, 16)] = out[...]

    def planes(k, carry):
        at = pl.ds(4 * k, 4)
        p_own[at], p_rim[at] = laplace(e_own, e_rim, 4 * k + 8, 4, 16, 48, shift_halves, True)
        return carry

    lax.fori_loop(0, 8, planes, 0)


def add_halo(slab, side, v_own, v_rim):
    lanes = lane_ids((8, LANES))
    edge, beyond = 4 + 20 * side, 28 * side
    empty = jnp.zeros((48, LANES), F32)
    for i in range(4):
        v_own[beyond + i] = empty
        v_rim[beyond + i] = empty
        v_own[edge + i] = empty
        v_rim[edge + i] = empty
        for q in range(5):
            v_own[edge + i, 4 + 8 * q : 12 + 8 * q, :] = slab[5 * i + q]
        for q in range(4):
            v_own[beyond + i, 8 + 8 * q : 16 + 8 * q, :] = slab[20 + 4 * i + q]
            rim = pltpu.roll(slab[36], (2 * LANES - 4 - 8 * (4 * i + q)) % LANES, 1)
            v_rim[edge + i, 8 + 8 * q : 16 + 8 * q, :] = jnp.where((lanes < 4) | (lanes >= LANES - 4), rim, 0.0)


def masks(flags, count, edge):
    rows = lax.broadcasted_iota(jnp.int32, (count, LANES), 0) - edge
    lanes = lane_ids((count, LANES))
    in_rows = (rows >= flags[3]) & (rows < flags[4])
    in_rim = ((lanes >= 64) & (flags[5] != 0)) | ((lanes < 64) & (flags[6] != 0))
    rows_one = jnp.where(in_rows, 1.0, 0.0)
    return rows_one, jnp.where(in_rim, rows_one, 0.0)


def steps(
    flags, shifts, p_own, p_rim, q_own, q_rim, at_q, v_own, v_rim, a_own, a_rim, b_own, b_rim, psi, one, two, three
):
    shift_halves = halves(shifts[...])
    last_halves = [m[:, :LANES] for m in shift_halves]

    def inside(x, edge):
        return jnp.where((x - edge >= flags[1]) & (x - edge < flags[2]), 1.0, 0.0)

    keep_own, keep_rim = masks(flags, 48, 8)

    def step_one(k, carry):
        x = one[0] + k
        keep = inside(x, 8)
        a_own[x] = (p_own[x] - STEP * v_own[x] * q_own[at_q + k, 16:64, :]) * (keep * keep_own)
        a_rim[x] = (p_rim[x] - STEP * v_rim[x] * q_rim[at_q + k, 16:64, :]) * (keep * keep_rim)
        return carry

    lax.fori_loop(0, one[1], step_one, 0, unroll=2)
    mid_own, mid_rim = masks(flags, 40, 4)

    def step_two(k, carry):
        x = two[0] + 4 * k
        at = pl.ds(x + 4, 4)
        fields = laplace(a_own, a_rim, x + 4, 4, 4, 40, shift_halves, True)
        for a, b, v, field, mask in (
            (a_own, b_own, v_own, fields[0], mid_own),
            (a_rim, b_rim, v_rim, fields[1], mid_rim),
        ):
            field = field - STEP * (v[at, 4:44, :] * a[at, 4:44, :])
            for i in range(4):
                b[x + i] = field[i] * (inside(x + i, 4) * mask)
        return carry

    lax.fori_loop(0, two[1] // 4, step_two, 0)

    def step_three(k, total):
        x = three[0] + 4 * k
        (field,) = laplace(b_own, b_rim, x + 4, 4, 4, 32, last_halves, False)
        field = field - STEP * (v_own[pl.ds(x + 8, 4), 8:40, :] * b_own[pl.ds(x + 4, 4), 4:36, :])
        psi[pl.ds(4 * k, 4)] = field
        return total + jnp.sum(field * field, axis=0)

    total = lax.fori_loop(0, three[1] // 4, step_three, jnp.zeros((32, LANES), F32))
    return jnp.sum(total, axis=0, keepdims=True)


def near_steps(
    flags, shifts, p_own, p_rim, q_own, q_rim, slab, v_far_own, v_far_rim, v_near_own, v_near_rim,
    a_kept_own, a_kept_rim, b_kept_own, b_kept_rim, psi, squares, v_own, v_rim, a_own, a_rim, b_own, b_rim,
):
    upper = flags[0]
    below = 1 - upper
    for v, far, near in ((v_own, v_far_own, v_near_own), (v_rim, v_far_rim, v_near_rim)):
        v[pl.ds(8 + 8 * upper, 8)] = far[...]
        v[pl.ds(8 + 8 * below, 8)] = near[...]
    add_halo(slab, below, v_own, v_rim)
    squares[...] = steps(
        flags, shifts, p_own, p_rim, q_own, q_rim, 8 * upper, v_own, v_rim, a_own, a_rim, b_own, b_rim, psi,
        (8 * below, 24), (8 * below, 16), (8 * below, 8),
    )
    a_kept_own[...] = a_own[pl.ds(8 + 8 * upper, 8)]
    a_kept_rim[...] = a_rim[pl.ds(8 + 8 * upper, 8)]
    b_kept_own[...] = b_own[8:16]
    b_kept_rim[...] = b_rim[8:16]


def far_steps(
    flags, shifts, p_own, p_rim, q_own, q_rim, slab, v_far_own, v_far_rim, near_squares,
    a_kept_own, a_kept_rim, b_kept_own, b_kept_rim, psi, squares, v_own, v_rim, a_own, a_rim, b_own, b_rim,
):
    upper = flags[0]
    below = 1 - upper
    v_own[pl.ds(8 + 8 * upper, 8)] = v_far_own[...]
    v_rim[pl.ds(8 + 8 * upper, 8)] = v_far_rim[...]
    a_own[pl.ds(8 + 8 * upper, 8)] = a_kept_own[...]
    a_rim[pl.ds(8 + 8 * upper, 8)] = a_kept_rim[...]
    b_own[8:16] = b_kept_own[...]
    b_rim[8:16] = b_kept_rim[...]
    add_halo(slab, upper, v_own, v_rim)
    squares[...] = near_squares[...] + steps(
        flags, shifts, p_own, p_rim, q_own, q_rim, 8 * below, v_own, v_rim, a_own, a_rim, b_own, b_rim, psi,
        (24 * upper, 8), (16 * upper, 8), (8 * upper, 8),
    )


def scale(count, flags, rows, near_psi, far_psi, out):
    total = jnp.sum(rows[...].reshape(-1, LANES), axis=0, keepdims=True)
    total = jnp.sum(total, axis=1, keepdims=True)
    factor = lax.rsqrt(total / count + 1e-06)
    upper = flags[0]
    out[pl.ds(8 * (1 - upper), 8)] = near_psi[...] * factor[None]
    out[pl.ds(8 * upper, 8)] = far_psi[...] * factor[None]


def swap_far(planes):
    count = lax.axis_size(GX)
    return lax.ppermute(planes, GX, [p for k in range(1, count - 1, 2) for p in ((k, k + 1), (k + 1, k))])


def swap_near(planes):
    return lax.ppermute(planes, GX, [(k, k ^ 1) for k in range(lax.axis_size(GX))])


def shift(head, tail, axis):
    ends = lax.axis_size(axis) - 1
    low = lax.ppermute(tail, axis, [(i, i + 1) for i in range(ends)])
    high = lax.ppermute(head, axis, [(i + 1, i) for i in range(ends)])
    return low, high


def spread(row, axes):
    count = lax.axis_size(axes)
    return lax.all_to_all(jnp.broadcast_to(row[None], (count, *row.shape)), axes, 0, 0, tiled=True)


def shards(wave, external, weights):
    at = [lax.axis_index(axis) for axis in (GX, "gy", "gz")]
    last = [at[d] == lax.axis_size(axis) - 1 for d, axis in enumerate((GX, "gy", "gz"))]
    far = 1 << 20
    flags = jnp.stack(
        [
            lax.axis_index("gx_2"),
            jnp.where(at[0] == 0, 0, -far),
            jnp.where(last[0], wave.shape[0], far),
            jnp.where(at[1] == 0, 0, -far),
            jnp.where(last[1], wave.shape[1], far),
            jnp.where(at[2] == 0, 0, 1),
            jnp.where(last[2], 0, 1),
        ]
    ).astype(jnp.int32)
    block = wave.shape
    outer = swap_far(wave)
    inner = swap_near(wave)
    head, tail = call(cut, [block] * 2, [], wave, external)
    low, high = shift(head, tail, "gy")
    smear_z, gather_z = call(bands, [(256, 256)] * 2, [], weights, scalars=1, flops=10**10)
    first, final, rows = call(
        pack_both,
        [(16, 24, LANES)] * 2 + [(16, 48, LANES)],
        [],
        wave, external, low, high,
        after=(inner, smear_z),
    )
    left, right = shift(first, final, "gz")
    i_rows = swap_near(rows)
    o_low, o_high = shift(*call(cut_outer, [(16, 24, LANES)] * 2, [], outer, after=(first, final)), "gy")
    first, final, sides = call(
        pack_outer, [(16, 16, LANES)] * 2 + [(16, 32, LANES)], [], outer, o_low, o_high, right, left
    )
    o_left, o_right = shift(first, final, "gz")
    i_sides = swap_near(sides)

    def twice(*shape):
        return [(*shape, LANES)] * 2

    own, rim, g_own, g_rim, s_own, s_rim, c_own, c_rim = call(
        prepare,
        twice(32, 80) + twice(16, 80) + twice(16, 64) + twice(16, 64),
        twice(32, 80) + twice(16, 80),
        flags, weights, smear_z, wave, low, high, right, left, inner, i_rows, i_sides,
        scalars=2,
    )
    halo = (low, high, right, left)
    out_own, out_rim, s_own, s_rim, far_corr, v_far_own, v_far_rim, outward = call(
        far_side,
        twice(16, 80) + twice(32, 64) + [(8, 32, LANES)] + twice(8, 48) + [(37, 8, LANES)],
        twice(16, 80) + twice(32, 80) + twice(16, 64) + twice(16, 80) + twice(8, 64) + twice(8, 48),
        flags, weights, smear_z, gather_z, external, *halo, outer, o_low, o_high, o_right, o_left,
        own, rim, g_own, g_rim, s_own, s_rim,
        scalars=2,
    )
    v_outer = swap_far(outward)
    corr, v_near_own, v_near_rim, inward = call(
        near_side,
        [block] + twice(8, 48) + [(37, 8, LANES)],
        [(8, 32, LANES)] + twice(8, 64) + twice(8, 48),
        flags, weights, gather_z, external, *halo, s_own, s_rim, c_own, c_rim, far_corr,
        scalars=2,
    )
    v_inner = swap_near(inward)
    shifts = jnp.asarray(ring_shifts())
    p_own, p_rim = call(
        first_step, twice(32, 48), twice(48, 80), flags, shifts, own, rim, out_own, out_rim, scalars=1, flops=10**10
    )
    scratch = twice(32, 48) * 2 + twice(24, 40)
    *kept, near_psi, squares = call(
        near_steps, twice(8, 48) + twice(8, 40) + [(8, 32, LANES), (1, LANES)], scratch,
        flags, shifts, p_own, p_rim, own, rim, v_inner, v_far_own, v_far_rim, v_near_own, v_near_rim,
        scalars=1,
    )
    far_psi, squares = call(
        far_steps, [(8, 32, LANES), (1, LANES)], scratch,
        flags, shifts, p_own, p_rim, out_own, out_rim, v_outer, v_far_own, v_far_rim, squares, *kept,
        scalars=1,
    )
    rows = spread(jnp.sum(spread(squares, RINGS[0]), axis=0), RINGS[1])
    count = float(wave.size * lax.axis_size(GX) * lax.axis_size("gy") * lax.axis_size("gz"))
    (wave_next,) = call(functools.partial(scale, count), [block], [], flags, rows, near_psi, far_psi, scalars=1)
    return (wave_next, corr)


def solution(mesh):
    torus = Mesh(
        mesh.devices.reshape(4, 2, 2, mesh.shape["gy"], mesh.shape["gz"]),
        ("gx_0", "gx_1", "gx_2", "gy", "gz"),
    )
    placed = (P(GX, "gy", "gz"), P(GX, "gy", "gz"), P())
    return jax.shard_map(
        shards,
        mesh=torus,
        in_specs=placed,
        out_specs=(P(GX, "gy", "gz"), P(GX, "gy", "gz")),
        check_vma=False,
    )
```

```python
import functools

import jax
import jax.numpy as jnp
import numpy as np
from jax import lax
from jax.experimental import pallas as pl
from jax.experimental.pallas import tpu as pltpu
from jax.sharding import Mesh
from jax.sharding import PartitionSpec as P

RINGS = (("gx_1", "gx_2", "gz"), ("gx_0", "gy"))
GX = ("gx_0", "gx_1", "gx_2")
LAP_COEF = (-205.0 / 72.0, 8.0 / 5.0, -1.0 / 5.0, 8.0 / 315.0, -1.0 / 560.0)
STEP = 0.08
F32 = jnp.float32
LANES = 128


def lane_ids(shape):
    return lax.broadcasted_iota(jnp.int32, shape, len(shape) - 1)


def pack(rows_of, count, cells, offset):
    lanes = lane_ids((8, LANES))
    first = last = None
    for q in range(count):
        at = offset + cells * q
        here = (lanes >= at) & (lanes < at + cells)
        rows = rows_of(q)
        head = pltpu.roll(rows, at, 1) if at else rows
        tail = pltpu.roll(rows, (at + cells) % LANES, 1)
        first = jnp.where(here, head, 0.0 if first is None else first)
        last = jnp.where(here, tail, 0.0 if last is None else last)
    return first, last


def unpack(right, left, at, cells):
    lanes = lane_ids((8, LANES))
    high = pltpu.roll(right, (LANES - at) % LANES, 1) if at % LANES else right
    low = pltpu.roll(left, (2 * LANES - cells - at) % LANES, 1)
    return jnp.where(lanes < cells, high, jnp.where(lanes >= LANES - cells, low, 0.0))


def skipping(body, start, count, *refs):
    body(*refs[:start], *refs[start + count :])


def call(body, outs, scratch, *args, scalars=0, flops=1000, after=()):
    specs = [pl.BlockSpec(memory_space=pltpu.SMEM)] * scalars
    specs += [pl.BlockSpec(memory_space=pltpu.VMEM)] * (len(args) - scalars)
    specs += [pl.BlockSpec(memory_space=pl.ANY)] * len(after)
    body = functools.partial(skipping, body, len(args), len(after))
    shapes = [jax.ShapeDtypeStruct(s, F32) for s in outs]
    nbytes = 4 * sum(a.size for a in args) + 4 * sum(s.size for s in shapes)
    return pl.pallas_call(
        body,
        out_shape=shapes,
        in_specs=specs,
        out_specs=[pl.BlockSpec(memory_space=pltpu.VMEM)] * len(outs),
        scratch_shapes=[pltpu.VMEM(s, F32) for s in scratch],
        compiler_params=pltpu.CompilerParams(vmem_limit_bytes=20 * 1024 * 1024),
        cost_estimate=pl.CostEstimate(flops=flops, bytes_accessed=nbytes, transcendentals=0),
    )(*args, *after)


def cut(wave, external, head, tail, same):
    same[...] = wave[...]
    head[:, 0:24, :] = wave[:, 0:24, :]
    head[:, 24:32, :] = external[:, 0:8, :]
    tail[:, 0:24, :] = wave[:, 8:32, :]
    tail[:, 24:32, :] = external[:, 24:32, :]


def cut_outer(outer, head, tail):
    head[...] = outer[:, 0:24, :]
    tail[...] = outer[:, 8:32, :]


def stacked(x, low, mid, high):
    def rows_of(q):
        for ref, start, stop in (low, mid, high):
            count = (stop - start) // 8
            if q < count:
                return ref[x, start + 8 * q : start + 8 * q + 8, :]
            q -= count

    return rows_of


def pack_cells(wave, low, high, first, last):
    def plane(x, carry):
        rows_of = stacked(x, (low, 0, 24), (wave, 0, 32), (high, 0, 24))
        for r in range(2):
            rows = slice(8 * r, 8 * r + 8)
            first[x, rows, :], last[x, rows, :] = pack(lambda q: rows_of(q + 5 * r), 5, 24, 0)
        return carry

    lax.fori_loop(0, 16, plane, 0, unroll=2)


def pack_both(wave, external, low, high, first, last, rows):
    pack_cells(wave, low, high, first, last)
    rows[:, 0:24, :] = low[:, 0:24, :]
    rows[:, 24:48, :] = high[:, 0:24, :]

    def plane(x, carry):
        rows_of = stacked(x, (low, 24, 32), (external, 0, 32), (high, 24, 32))
        first[x, 16:24, :], last[x, 16:24, :] = pack(rows_of, 6, 8, 0)
        return carry

    lax.fori_loop(0, 16, plane, 0, unroll=2)


def pack_outer(wave, low, high, right, left, first, last, sides):
    pack_cells(wave, low, high, first, last)
    sides[:, 0:16, :] = right[:, 0:16, :]
    sides[:, 16:32, :] = left[:, 0:16, :]


def fill(own, rim, base, mid, low, high, right, left):
    def plane(x, carry):
        own[base + x, 0:24, :] = low[x, 0:24, :]
        own[base + x, 24:56, :] = mid[x]
        own[base + x, 56:80, :] = high[x, 0:24, :]
        for g in range(10):
            rows = slice(8 * (g // 5), 8 * (g // 5) + 8)
            rim[base + x, 8 * g : 8 * g + 8, :] = unpack(right[x, rows, :], left[x, rows, :], 24 * (g % 5), 24)
        return carry

    lax.fori_loop(0, 16, plane, 0, unroll=4)


def halves(x):
    top = x.astype(jnp.bfloat16)
    return top, (x - top.astype(F32)).astype(jnp.bfloat16)


def times(x, matrix_halves):
    top, rest = halves(x)
    big, small = matrix_halves
    dot = functools.partial(jnp.dot, preferred_element_type=F32)
    return dot(top, big) + (dot(top, small) + dot(rest, big))


def slide(src, base, dst, taps, groups):
    count = dst.shape[0]

    def column(g, carry):
        rows = pl.ds(pl.multiple_of(8 * g, 8), 8)
        sums = {}
        for j in range(count + 16):
            value = src[base + j, rows, :]
            for a in range(17):
                i = j - a
                if 0 <= i < count:
                    term = taps[a] * value
                    sums[i] = sums[i] + term if a else term
            if j >= 16:
                dst[j - 16, rows, :] = sums.pop(j - 16)
        return carry

    lax.fori_loop(0, groups, column, 0)


def along_rows(src, x, taps, count):
    total = taps[0] * src[x, 0:count, :]
    for b in range(1, 17):
        total = total + taps[b] * src[x, b : b + count, :]
    return total


def along_z(own, rim, g_own, g_rim, base, spread_halves, start=None):
    start = base if start is None else start

    def chunk(k, carry):
        planes = pl.ds(start + 8 * k, 8)
        a = own[planes].reshape(640, LANES)
        b = rim[planes].reshape(640, LANES)
        out = times(jnp.concatenate([a * a, b * b], axis=1), spread_halves)
        planes = pl.ds(base + 8 * k, 8)
        g_own[planes] = out[:, :LANES].reshape(8, 80, LANES)
        g_rim[planes] = out[:, LANES:].reshape(8, 80, LANES)
        return carry

    lax.fori_loop(0, 2, chunk, 0)


def sources(weights, field, at, g_own, g_rim, base, s_own, s_rim, to, c_own, c_rim, h_own, h_rim):
    x_taps = [weights[0, a] for a in range(17)]
    slide(g_own, base, h_own, x_taps, 10)
    slide(g_rim, base, h_rim, x_taps, 10)
    offset = lax.broadcasted_iota(jnp.int32, (64, 80), 1) - lax.broadcasted_iota(jnp.int32, (64, 80), 0)
    rows = jnp.zeros((64, 80), F32)
    for tap in range(17):
        rows = jnp.where(offset == tap, weights[1, tap], rows)
    top, rest = halves(rows)
    stack = jnp.concatenate([top, rest], axis=0)
    dot = functools.partial(jnp.dot, preferred_element_type=F32)

    def source(k, carry):
        for i in range(4):
            x = 4 * k + i
            for h, e, s, c in ((h_own, field[0], s_own, c_own), (h_rim, field[1], s_rim, c_rim)):
                big, small = halves(h[x])
                both = dot(stack, big)
                coarse = both[:64] + (both[64:] + dot(top, small))
                wave = e[at + x, 8:72, :]
                density = wave * wave
                s[to + x] = -1.0 * density * coarse + 0.5 * density * coarse * coarse
                c[x] = coarse
        return carry

    lax.fori_loop(0, 4, source, 0)


def band(weights, flip):
    def places(dim):
        at = lax.broadcasted_iota(jnp.int32, (256, 256), dim)
        return jnp.where(at < 192, at, at - 256)

    start, end = places(0), places(1)
    margin = 8 if flip else 16
    offset = (end - start if flip else start - end) + 8
    used = (end >= -margin) & (end < LANES + margin) & (start >= -margin - 8) & (start < LANES + margin + 8)
    offset = jnp.where(used, offset, -1)
    matrix = jnp.zeros((256, 256), F32)
    for tap in range(17):
        matrix = jnp.where(offset == tap, weights[2, tap], matrix)
    return matrix


def bands(weights, spread, gather, token):
    token[...] = jnp.zeros_like(token)
    spread[...] = band(weights, False)
    gather[...] = band(weights, True)


def prepare(
    flags, weights, spread, wave, low, high, right, left, inner, i_rows, i_sides,
    own, rim, g_own, g_rim, s_own, s_rim, c_own, c_rim, k_own, k_rim, h_own, h_rim,
):
    spread_halves = halves(spread[...])
    upper = flags[0]
    mine, other = 16 * upper, 16 * (1 - upper)
    i_low, i_high = i_rows.at[:, 0:24, :], i_rows.at[:, 24:48, :]
    i_right, i_left = i_sides.at[:, 0:16, :], i_sides.at[:, 16:32, :]
    fill(own, rim, mine, wave, low, high, right, left)
    fill(own, rim, other, inner, i_low, i_high, i_right, i_left)
    along_z(own, rim, k_own, k_rim, 0, spread_halves)
    along_z(own, rim, k_own, k_rim, 16, spread_halves)
    g_own[...] = k_own[pl.ds(mine, 16)]
    g_rim[...] = k_rim[pl.ds(mine, 16)]
    sources(weights, (own, rim), 8, k_own, k_rim, 0, s_own, s_rim, 0, c_own, c_rim, h_own, h_rim)


def potentials(
    side, weights, gather, external, low, high, right, left, s_own, s_rim, c_own, c_rim, at_c,
    corr, v_own, v_rim, slab, t_own, t_rim, u_own, u_rim,
):
    x_taps = [weights[0, 16 - a] for a in range(17)]
    y_taps = [weights[1, 16 - a] for a in range(17)]
    base = 8 * side
    slide(s_own, base, t_own, x_taps, 8)
    slide(s_rim, base, t_rim, x_taps, 8)

    def back(x, carry):
        u_own[x] = along_rows(t_own, x, y_taps, 48)
        u_rim[x] = along_rows(t_rim, x, y_taps, 48)
        return carry

    lax.fori_loop(0, 8, back, 0)
    both = jnp.concatenate([u_own[...].reshape(384, LANES), u_rim[...].reshape(384, LANES)], axis=1)
    smeared = times(both, halves(gather[...]))
    planes = pl.ds(base, 8)
    for c, v, part in ((c_own, v_own, smeared[:, :LANES]), (c_rim, v_rim, smeared[:, LANES:])):
        coarse = c[pl.ds(at_c, 8), 8:56, :]
        v[...] = -0.5 * coarse * coarse + 0.5 / 3.0 * coarse * coarse * coarse + part.reshape(8, 48, LANES)
    corr[...] = v_own[:, 8:40, :]
    v_own[:, 0:8, :] += low[planes, 24:32, :]
    v_own[:, 8:40, :] += external[planes]
    v_own[:, 40:48, :] += high[planes, 24:32, :]
    for x in range(8):
        for q in range(6):
            v_rim[x, 8 * q : 8 * q + 8, :] += unpack(right[base + x, 16:24, :], left[base + x, 16:24, :], 8 * q, 8)

    lanes = lane_ids((8, LANES))
    edge, beyond = 4 * side, 4 - 4 * side
    rims = jnp.zeros((8, LANES), F32)
    for i in range(4):
        for q in range(5):
            slab[5 * i + q] = v_own[edge + i, 4 + 8 * q : 12 + 8 * q, :]
        for q in range(4):
            slab[20 + 4 * i + q] = v_own[beyond + i, 8 + 8 * q : 16 + 8 * q, :]
            at = 8 * (4 * i + q)
            these = (lanes >= at) & (lanes < at + 8)
            rims = jnp.where(these, pltpu.roll(v_rim[edge + i, 8 + 8 * q : 16 + 8 * q, :], (at + 4) % LANES, 1), rims)
    slab[36] = rims


def far_side(
    flags, weights, spread, gather, external, low, high, right, left, outer, o_low, o_high, o_right, o_left,
    own, rim, g_own, g_rim, s_own, s_rim, out_own, out_rim, s_all_own, s_all_rim, corr, v_own, v_rim, slab,
    e_own, e_rim, k_own, k_rim, c_own, c_rim, h_own, h_rim, t_own, t_rim, u_own, u_rim,
):
    upper = flags[0]
    below = 1 - upper
    fill(out_own, out_rim, 0, outer, o_low, o_high, o_right, o_left)
    along_z(out_own, out_rim, k_own, k_rim, 16 * upper, halves(spread[...]), 0)
    mine = pl.ds(16 * below, 16)
    k_own[mine] = g_own[...]
    k_rim[mine] = g_rim[...]
    for e, out, field in ((e_own, out_own, own), (e_rim, out_rim, rim)):
        e[pl.ds(8 * upper, 8)] = out[pl.ds(8 * below, 8)]
        e[pl.ds(8 * below, 8)] = field[pl.ds(24 * upper, 8)]
    for s_all, s in ((s_all_own, s_own), (s_all_rim, s_rim)):
        s_all[pl.ds(16 * below, 16)] = s[...]
    sources(
        weights, (e_own, e_rim), 0, k_own, k_rim, 0, s_all_own, s_all_rim, 16 * upper, c_own, c_rim, h_own, h_rim
    )
    potentials(
        upper, weights, gather, external, low, high, right, left, s_all_own, s_all_rim, c_own, c_rim, 8 * below,
        corr, v_own, v_rim, slab, t_own, t_rim, u_own, u_rim,
    )


def near_side(
    flags, weights, gather, external, low, high, right, left, s_own, s_rim, c_own, c_rim, far_corr,
    corr, v_own, v_rim, slab, near_corr, t_own, t_rim, u_own, u_rim,
):
    upper = flags[0]
    below = 1 - upper
    potentials(
        below, weights, gather, external, low, high, right, left, s_own, s_rim, c_own, c_rim, 8 * upper,
        near_corr, v_own, v_rim, slab, t_own, t_rim, u_own, u_rim,
    )
    corr[pl.ds(8 * below, 8)] = near_corr[...]
    corr[pl.ds(8 * upper, 8)] = far_corr[...]


def laplace(own, rim, x, count, start, rows, shifts, with_rim):
    planes = pl.ds(x, count)
    here = slice(start, start + rows)
    centers = own[planes, here, :], rim[planes, here, :]
    flat = [c.reshape(count * rows, LANES) for c in centers]
    shifted = times(jnp.concatenate(flat, axis=1), shifts)
    answers = []
    for ref in range(2 if with_rim else 1):
        field = (own, rim)[ref]
        part = shifted[:, LANES * ref : LANES * ref + LANES].reshape(count, rows, LANES)
        total = (1.0 + 0.5 * STEP * 3.0 * LAP_COEF[0]) * centers[ref] + part
        for k in range(1, 5):
            near = field[pl.ds(x + k, count), here, :] + field[pl.ds(x - k, count), here, :]
            near = near + (field[planes, start + k : start + k + rows, :] + field[planes, start - k : start - k + rows, :])
            total = total + (0.5 * STEP * LAP_COEF[k]) * near
        answers.append(total)
    return answers


def ring_shifts():
    gap = np.abs(np.arange(256)[:, None] - np.arange(256)[None, :])
    gap = np.minimum(gap, 256 - gap)
    matrix = np.zeros((256, 256), np.float32)
    for k in range(1, 5):
        matrix[gap == k] = 0.5 * STEP * LAP_COEF[k]
    return matrix


def first_step(flags, shifts, own, rim, out_own, out_rim, p_own, p_rim, e_own, e_rim):
    shift_halves = halves(shifts[...])
    upper = flags[0]
    for e, field, out in ((e_own, own, out_own), (e_rim, rim, out_rim)):
        e[pl.ds(16 * (1 - upper), 32)] = field[...]
        e[pl.ds(32 * upper, 16)] = out[...]

    def planes(k, carry):
        at = pl.ds(4 * k, 4)
        p_own[at], p_rim[at] = laplace(e_own, e_rim, 4 * k + 8, 4, 16, 48, shift_halves, True)
        return carry

    lax.fori_loop(0, 8, planes, 0)


def add_halo(slab, side, v_own, v_rim):
    lanes = lane_ids((8, LANES))
    edge, beyond = 4 + 20 * side, 28 * side
    empty = jnp.zeros((48, LANES), F32)
    for i in range(4):
        v_own[beyond + i] = empty
        v_rim[beyond + i] = empty
        v_own[edge + i] = empty
        v_rim[edge + i] = empty
        for q in range(5):
            v_own[edge + i, 4 + 8 * q : 12 + 8 * q, :] = slab[5 * i + q]
        for q in range(4):
            v_own[beyond + i, 8 + 8 * q : 16 + 8 * q, :] = slab[20 + 4 * i + q]
            rim = pltpu.roll(slab[36], (2 * LANES - 4 - 8 * (4 * i + q)) % LANES, 1)
            v_rim[edge + i, 8 + 8 * q : 16 + 8 * q, :] = jnp.where((lanes < 4) | (lanes >= LANES - 4), rim, 0.0)


def masks(flags, count, edge):
    rows = lax.broadcasted_iota(jnp.int32, (count, LANES), 0) - edge
    lanes = lane_ids((count, LANES))
    in_rows = (rows >= flags[3]) & (rows < flags[4])
    in_rim = ((lanes >= 64) & (flags[5] != 0)) | ((lanes < 64) & (flags[6] != 0))
    rows_one = jnp.where(in_rows, 1.0, 0.0)
    return rows_one, jnp.where(in_rim, rows_one, 0.0)


def steps(
    flags, shifts, p_own, p_rim, q_own, q_rim, at_q, v_own, v_rim, a_own, a_rim, b_own, b_rim, psi, one, two, three
):
    shift_halves = halves(shifts[...])
    last_halves = [m[:, :LANES] for m in shift_halves]

    def inside(x, edge):
        return jnp.where((x - edge >= flags[1]) & (x - edge < flags[2]), 1.0, 0.0)

    keep_own, keep_rim = masks(flags, 48, 8)

    def step_one(k, carry):
        x = one[0] + k
        keep = inside(x, 8)
        a_own[x] = (p_own[x] - STEP * v_own[x] * q_own[at_q + k, 16:64, :]) * (keep * keep_own)
        a_rim[x] = (p_rim[x] - STEP * v_rim[x] * q_rim[at_q + k, 16:64, :]) * (keep * keep_rim)
        return carry

    lax.fori_loop(0, one[1], step_one, 0, unroll=2)
    mid_own, mid_rim = masks(flags, 40, 4)

    def step_two(k, carry):
        x = two[0] + 4 * k
        at = pl.ds(x + 4, 4)
        fields = laplace(a_own, a_rim, x + 4, 4, 4, 40, shift_halves, True)
        for a, b, v, field, mask in (
            (a_own, b_own, v_own, fields[0], mid_own),
            (a_rim, b_rim, v_rim, fields[1], mid_rim),
        ):
            field = field - STEP * (v[at, 4:44, :] * a[at, 4:44, :])
            for i in range(4):
                b[x + i] = field[i] * (inside(x + i, 4) * mask)
        return carry

    lax.fori_loop(0, two[1] // 4, step_two, 0)

    def step_three(k, total):
        x = three[0] + 4 * k
        (field,) = laplace(b_own, b_rim, x + 4, 4, 4, 32, last_halves, False)
        field = field - STEP * (v_own[pl.ds(x + 8, 4), 8:40, :] * b_own[pl.ds(x + 4, 4), 4:36, :])
        psi[pl.ds(4 * k, 4)] = field
        return total + jnp.sum(field * field, axis=0)

    total = lax.fori_loop(0, three[1] // 4, step_three, jnp.zeros((32, LANES), F32))
    return jnp.sum(total, axis=0, keepdims=True)


def near_steps(
    flags, shifts, p_own, p_rim, q_own, q_rim, slab, v_far_own, v_far_rim, v_near_own, v_near_rim,
    a_kept_own, a_kept_rim, b_kept_own, b_kept_rim, psi, squares, v_own, v_rim, a_own, a_rim, b_own, b_rim,
):
    upper = flags[0]
    below = 1 - upper
    for v, far, near in ((v_own, v_far_own, v_near_own), (v_rim, v_far_rim, v_near_rim)):
        v[pl.ds(8 + 8 * upper, 8)] = far[...]
        v[pl.ds(8 + 8 * below, 8)] = near[...]
    add_halo(slab, below, v_own, v_rim)
    squares[...] = steps(
        flags, shifts, p_own, p_rim, q_own, q_rim, 8 * upper, v_own, v_rim, a_own, a_rim, b_own, b_rim, psi,
        (8 * below, 24), (8 * below, 16), (8 * below, 8),
    )
    a_kept_own[...] = a_own[pl.ds(8 + 8 * upper, 8)]
    a_kept_rim[...] = a_rim[pl.ds(8 + 8 * upper, 8)]
    b_kept_own[...] = b_own[8:16]
    b_kept_rim[...] = b_rim[8:16]


def far_steps(
    flags, shifts, p_own, p_rim, q_own, q_rim, slab, v_far_own, v_far_rim, near_squares,
    a_kept_own, a_kept_rim, b_kept_own, b_kept_rim, psi, squares, v_own, v_rim, a_own, a_rim, b_own, b_rim,
):
    upper = flags[0]
    below = 1 - upper
    v_own[pl.ds(8 + 8 * upper, 8)] = v_far_own[...]
    v_rim[pl.ds(8 + 8 * upper, 8)] = v_far_rim[...]
    a_own[pl.ds(8 + 8 * upper, 8)] = a_kept_own[...]
    a_rim[pl.ds(8 + 8 * upper, 8)] = a_kept_rim[...]
    b_own[8:16] = b_kept_own[...]
    b_rim[8:16] = b_kept_rim[...]
    add_halo(slab, upper, v_own, v_rim)
    squares[...] = near_squares[...] + steps(
        flags, shifts, p_own, p_rim, q_own, q_rim, 8 * below, v_own, v_rim, a_own, a_rim, b_own, b_rim, psi,
        (24 * upper, 8), (16 * upper, 8), (8 * upper, 8),
    )


def scale(count, flags, rows, near_psi, far_psi, out):
    total = jnp.sum(rows[...].reshape(-1, LANES), axis=0, keepdims=True)
    total = jnp.sum(total, axis=1, keepdims=True)
    factor = lax.rsqrt(total / count + 1e-06)
    upper = flags[0]
    out[pl.ds(8 * (1 - upper), 8)] = near_psi[...] * factor[None]
    out[pl.ds(8 * upper, 8)] = far_psi[...] * factor[None]


def swap_far(planes):
    count = lax.axis_size(GX)
    return lax.ppermute(planes, GX, [p for k in range(1, count - 1, 2) for p in ((k, k + 1), (k + 1, k))])


def swap_near(planes):
    return lax.ppermute(planes, GX, [(k, k ^ 1) for k in range(lax.axis_size(GX))])


def shift(head, tail, axis):
    ends = lax.axis_size(axis) - 1
    low = lax.ppermute(tail, axis, [(i, i + 1) for i in range(ends)])
    high = lax.ppermute(head, axis, [(i + 1, i) for i in range(ends)])
    return low, high


def spread(row, axes):
    count = lax.axis_size(axes)
    return lax.all_to_all(jnp.broadcast_to(row[None], (count, *row.shape)), axes, 0, 0, tiled=True)


def shards(wave, external, weights):
    at = [lax.axis_index(axis) for axis in (GX, "gy", "gz")]
    last = [at[d] == lax.axis_size(axis) - 1 for d, axis in enumerate((GX, "gy", "gz"))]
    far = 1 << 20
    flags = jnp.stack(
        [
            lax.axis_index("gx_2"),
            jnp.where(at[0] == 0, 0, -far),
            jnp.where(last[0], wave.shape[0], far),
            jnp.where(at[1] == 0, 0, -far),
            jnp.where(last[1], wave.shape[1], far),
            jnp.where(at[2] == 0, 0, 1),
            jnp.where(last[2], 0, 1),
        ]
    ).astype(jnp.int32)
    block = wave.shape
    outer = swap_far(wave)
    head, tail, same = call(cut, [block] * 3, [], wave, external)
    inner = swap_near(same)
    low, high = shift(head, tail, "gy")
    smear_z, gather_z, token = call(bands, [(256, 256)] * 2 + [(8, LANES)], [], weights, scalars=1, flops=5 * 10**9)
    first, final, rows = call(
        pack_both,
        [(16, 24, LANES)] * 2 + [(16, 48, LANES)],
        [],
        wave, external, low, high,
        after=(inner, token),
    )
    left, right = shift(first, final, "gz")
    i_rows = swap_near(rows)
    o_low, o_high = shift(*call(cut_outer, [(16, 24, LANES)] * 2, [], outer, after=(first, final)), "gy")
    first, final, sides = call(
        pack_outer, [(16, 16, LANES)] * 2 + [(16, 32, LANES)], [], outer, o_low, o_high, right, left
    )
    o_left, o_right = shift(first, final, "gz")
    i_sides = swap_near(sides)

    def twice(*shape):
        return [(*shape, LANES)] * 2

    own, rim, g_own, g_rim, s_own, s_rim, c_own, c_rim = call(
        prepare,
        twice(32, 80) + twice(16, 80) + twice(16, 64) + twice(16, 64),
        twice(32, 80) + twice(16, 80),
        flags, weights, smear_z, wave, low, high, right, left, inner, i_rows, i_sides,
        scalars=2,
    )
    halo = (low, high, right, left)
    out_own, out_rim, s_own, s_rim, far_corr, v_far_own, v_far_rim, outward = call(
        far_side,
        twice(16, 80) + twice(32, 64) + [(8, 32, LANES)] + twice(8, 48) + [(37, 8, LANES)],
        twice(16, 80) + twice(32, 80) + twice(16, 64) + twice(16, 80) + twice(8, 64) + twice(8, 48),
        flags, weights, smear_z, gather_z, external, *halo, outer, o_low, o_high, o_right, o_left,
        own, rim, g_own, g_rim, s_own, s_rim,
        scalars=2,
    )
    v_outer = swap_far(outward)
    shifts = jnp.asarray(ring_shifts())

    def beside(*args):
        corr, v_near_own, v_near_rim, inward = call(
            near_side,
            [block] + twice(8, 48) + [(37, 8, LANES)],
            [(8, 32, LANES)] + twice(8, 64) + twice(8, 48),
            flags, weights, gather_z, external, *halo, s_own, s_rim, c_own, c_rim, far_corr,
            scalars=2,
        )
        v_inner = swap_near(inward)
        p_own, p_rim = call(
            first_step, twice(32, 48), twice(48, 80), flags, shifts, own, rim, out_own, out_rim, scalars=1
        )
        return corr, v_near_own, v_near_rim, v_inner, p_own, p_rim

    def nothing(*args):
        shapes = [block, *twice(8, 48), (37, 8, LANES), *twice(32, 48)]
        return tuple(jnp.zeros(shape, F32) for shape in shapes)

    corr, v_near_own, v_near_rim, v_inner, p_own, p_rim = lax.cond(flags[0] >= 0, beside, nothing)
    scratch = twice(32, 48) * 2 + twice(24, 40)
    *kept, near_psi, squares = call(
        near_steps, twice(8, 48) + twice(8, 40) + [(8, 32, LANES), (1, LANES)], scratch,
        flags, shifts, p_own, p_rim, own, rim, v_inner, v_far_own, v_far_rim, v_near_own, v_near_rim,
        scalars=1,
    )
    far_psi, squares = call(
        far_steps, [(8, 32, LANES), (1, LANES)], scratch,
        flags, shifts, p_own, p_rim, out_own, out_rim, v_outer, v_far_own, v_far_rim, squares, *kept,
        scalars=1,
    )
    rows = spread(jnp.sum(spread(squares, RINGS[0]), axis=0), RINGS[1])
    count = float(wave.size * lax.axis_size(GX) * lax.axis_size("gy") * lax.axis_size("gz"))
    (wave_next,) = call(functools.partial(scale, count), [block], [], flags, rows, near_psi, far_psi, scalars=1)
    return (wave_next, corr)


def solution(mesh):
    torus = Mesh(
        mesh.devices.reshape(4, 2, 2, mesh.shape["gy"], mesh.shape["gz"]),
        ("gx_0", "gx_1", "gx_2", "gy", "gz"),
    )
    placed = (P(GX, "gy", "gz"), P(GX, "gy", "gz"), P())
    return jax.shard_map(
        shards,
        mesh=torus,
        in_specs=placed,
        out_specs=(P(GX, "gy", "gz"), P(GX, "gy", "gz")),
        check_vma=False,
    )
```

```python
import functools

import jax
import jax.numpy as jnp
import numpy as np
from jax import lax
from jax.experimental import pallas as pl
from jax.experimental.pallas import tpu as pltpu
from jax.sharding import Mesh
from jax.sharding import PartitionSpec as P

RINGS = (("gx_1", "gx_2", "gz"), ("gx_0", "gy"))
GX = ("gx_0", "gx_1", "gx_2")
LAP_COEF = (-205.0 / 72.0, 8.0 / 5.0, -1.0 / 5.0, 8.0 / 315.0, -1.0 / 560.0)
STEP = 0.08
F32 = jnp.float32
LANES = 128


def lane_ids(shape):
    return lax.broadcasted_iota(jnp.int32, shape, len(shape) - 1)


def pack(rows_of, count, cells, offset):
    lanes = lane_ids((8, LANES))
    first = last = None
    for q in range(count):
        at = offset + cells * q
        here = (lanes >= at) & (lanes < at + cells)
        rows = rows_of(q)
        head = pltpu.roll(rows, at, 1) if at else rows
        tail = pltpu.roll(rows, (at + cells) % LANES, 1)
        first = jnp.where(here, head, 0.0 if first is None else first)
        last = jnp.where(here, tail, 0.0 if last is None else last)
    return first, last


def unpack(right, left, at, cells):
    lanes = lane_ids((8, LANES))
    high = pltpu.roll(right, (LANES - at) % LANES, 1) if at % LANES else right
    low = pltpu.roll(left, (2 * LANES - cells - at) % LANES, 1)
    return jnp.where(lanes < cells, high, jnp.where(lanes >= LANES - cells, low, 0.0))


def skipping(body, start, count, *refs):
    body(*refs[:start], *refs[start + count :])


def call(body, outs, scratch, *args, scalars=0, flops=1000, after=()):
    specs = [pl.BlockSpec(memory_space=pltpu.SMEM)] * scalars
    specs += [pl.BlockSpec(memory_space=pltpu.VMEM)] * (len(args) - scalars)
    specs += [pl.BlockSpec(memory_space=pl.ANY)] * len(after)
    body = functools.partial(skipping, body, len(args), len(after))
    shapes = [jax.ShapeDtypeStruct(s, F32) for s in outs]
    nbytes = 4 * sum(a.size for a in args) + 4 * sum(s.size for s in shapes)
    return pl.pallas_call(
        body,
        out_shape=shapes,
        in_specs=specs,
        out_specs=[pl.BlockSpec(memory_space=pltpu.VMEM)] * len(outs),
        scratch_shapes=[pltpu.VMEM(s, F32) for s in scratch],
        compiler_params=pltpu.CompilerParams(vmem_limit_bytes=20 * 1024 * 1024),
        cost_estimate=pl.CostEstimate(flops=flops, bytes_accessed=nbytes, transcendentals=0),
    )(*args, *after)


def cut(wave, external, head, tail, same):
    same[...] = wave[...]
    head[:, 0:24, :] = wave[:, 0:24, :]
    head[:, 24:32, :] = external[:, 0:8, :]
    tail[:, 0:24, :] = wave[:, 8:32, :]
    tail[:, 24:32, :] = external[:, 24:32, :]


def cut_outer(outer, head, tail):
    head[...] = outer[:, 0:24, :]
    tail[...] = outer[:, 8:32, :]


def stacked(x, low, mid, high):
    def rows_of(q):
        for ref, start, stop in (low, mid, high):
            count = (stop - start) // 8
            if q < count:
                return ref[x, start + 8 * q : start + 8 * q + 8, :]
            q -= count

    return rows_of


def pack_cells(wave, low, high, first, last):
    def plane(x, carry):
        rows_of = stacked(x, (low, 0, 24), (wave, 0, 32), (high, 0, 24))
        for r in range(2):
            rows = slice(8 * r, 8 * r + 8)
            first[x, rows, :], last[x, rows, :] = pack(lambda q: rows_of(q + 5 * r), 5, 24, 0)
        return carry

    lax.fori_loop(0, 16, plane, 0, unroll=2)


def pack_both(wave, external, low, high, first, last, rows):
    pack_cells(wave, low, high, first, last)
    rows[:, 0:24, :] = low[:, 0:24, :]
    rows[:, 24:48, :] = high[:, 0:24, :]

    for j in range(8):
        rows_of = [stacked(2 * j + i, (low, 24, 32), (external, 0, 32), (high, 24, 32)) for i in range(2)]
        one, two = pack(rows_of[0], 6, 8, 0), pack(rows_of[1], 6, 8, 48)
        here = 16 + j // 2, slice(8 * (j % 2), 8 * (j % 2) + 8)
        first[here] = one[0] + two[0]
        last[here] = one[1] + two[1]


def pack_outer(wave, low, high, right, left, first, last, sides):
    pack_cells(wave, low, high, first, last)
    sides[:, 0:16, :] = right[0:16]
    sides[:, 16:32, :] = left[0:16]


def fill(own, rim, base, mid, low, high, right, left):
    def plane(x, carry):
        own[base + x, 0:24, :] = low[x, 0:24, :]
        own[base + x, 24:56, :] = mid[x]
        own[base + x, 56:80, :] = high[x, 0:24, :]
        for g in range(10):
            rows = slice(8 * (g // 5), 8 * (g // 5) + 8)
            rim[base + x, 8 * g : 8 * g + 8, :] = unpack(right[x, rows, :], left[x, rows, :], 24 * (g % 5), 24)
        return carry

    lax.fori_loop(0, 16, plane, 0, unroll=4)


def halves(x):
    top = x.astype(jnp.bfloat16)
    return top, (x - top.astype(F32)).astype(jnp.bfloat16)


def times(x, matrix_halves):
    top, rest = halves(x)
    big, small = matrix_halves
    dot = functools.partial(jnp.dot, preferred_element_type=F32)
    return dot(top, big) + (dot(top, small) + dot(rest, big))


def slide(src, base, dst, taps, groups):
    count = dst.shape[0]

    def column(g, carry):
        rows = pl.ds(pl.multiple_of(8 * g, 8), 8)
        sums = {}
        for j in range(count + 16):
            value = src[base + j, rows, :]
            for a in range(17):
                i = j - a
                if 0 <= i < count:
                    term = taps[a] * value
                    sums[i] = sums[i] + term if a else term
            if j >= 16:
                dst[j - 16, rows, :] = sums.pop(j - 16)
        return carry

    lax.fori_loop(0, groups, column, 0)


def along_rows(src, x, taps, count):
    total = taps[0] * src[x, 0:count, :]
    for b in range(1, 17):
        total = total + taps[b] * src[x, b : b + count, :]
    return total


def along_z(own, rim, g_own, g_rim, base, spread_halves, start=None):
    start = base if start is None else start

    def chunk(k, carry):
        planes = pl.ds(start + 8 * k, 8)
        a = own[planes].reshape(640, LANES)
        b = rim[planes].reshape(640, LANES)
        out = times(jnp.concatenate([a * a, b * b], axis=1), spread_halves)
        planes = pl.ds(base + 8 * k, 8)
        g_own[planes] = out[:, :LANES].reshape(8, 80, LANES)
        g_rim[planes] = out[:, LANES:].reshape(8, 80, LANES)
        return carry

    lax.fori_loop(0, 2, chunk, 0)


def sources(weights, field, at, g_own, g_rim, base, s_own, s_rim, to, c_own, c_rim, h_own, h_rim):
    x_taps = [weights[0, a] for a in range(17)]
    slide(g_own, base, h_own, x_taps, 10)
    slide(g_rim, base, h_rim, x_taps, 10)
    offset = lax.broadcasted_iota(jnp.int32, (64, 80), 1) - lax.broadcasted_iota(jnp.int32, (64, 80), 0)
    rows = jnp.zeros((64, 80), F32)
    for tap in range(17):
        rows = jnp.where(offset == tap, weights[1, tap], rows)
    top, rest = halves(rows)
    stack = jnp.concatenate([top, rest], axis=0)
    dot = functools.partial(jnp.dot, preferred_element_type=F32)

    def source(k, carry):
        for i in range(4):
            x = 4 * k + i
            for h, e, s, c in ((h_own, field[0], s_own, c_own), (h_rim, field[1], s_rim, c_rim)):
                big, small = halves(h[x])
                both = dot(stack, big)
                coarse = both[:64] + (both[64:] + dot(top, small))
                wave = e[at + x, 8:72, :]
                density = wave * wave
                s[to + x] = -1.0 * density * coarse + 0.5 * density * coarse * coarse
                c[x] = coarse
        return carry

    lax.fori_loop(0, 4, source, 0)


def band(weights, flip):
    def places(dim):
        at = lax.broadcasted_iota(jnp.int32, (256, 256), dim)
        return jnp.where(at < 192, at, at - 256)

    start, end = places(0), places(1)
    margin = 8 if flip else 16
    offset = (end - start if flip else start - end) + 8
    used = (end >= -margin) & (end < LANES + margin) & (start >= -margin - 8) & (start < LANES + margin + 8)
    offset = jnp.where(used, offset, -1)
    matrix = jnp.zeros((256, 256), F32)
    for tap in range(17):
        matrix = jnp.where(offset == tap, weights[2, tap], matrix)
    return matrix


def bands(weights, spread, gather, token):
    token[...] = jnp.zeros_like(token)
    spread[...] = band(weights, False)
    gather[...] = band(weights, True)


def prepare(
    flags, weights, spread, wave, low, high, right, left, inner, i_rows, i_sides,
    own, rim, g_own, g_rim, s_own, s_rim, c_own, c_rim, k_own, k_rim, h_own, h_rim,
):
    spread_halves = halves(spread[...])
    upper = flags[0]
    mine, other = 16 * upper, 16 * (1 - upper)
    i_low, i_high = i_rows.at[:, 0:24, :], i_rows.at[:, 24:48, :]
    i_right, i_left = i_sides.at[:, 0:16, :], i_sides.at[:, 16:32, :]
    fill(own, rim, mine, wave, low, high, right, left)
    fill(own, rim, other, inner, i_low, i_high, i_right, i_left)
    along_z(own, rim, k_own, k_rim, 0, spread_halves)
    along_z(own, rim, k_own, k_rim, 16, spread_halves)
    g_own[...] = k_own[pl.ds(mine, 16)]
    g_rim[...] = k_rim[pl.ds(mine, 16)]
    sources(weights, (own, rim), 8, k_own, k_rim, 0, s_own, s_rim, 0, c_own, c_rim, h_own, h_rim)


def potentials(
    side, weights, gather, external, low, high, right, left, s_own, s_rim, c_own, c_rim, at_c,
    corr, v_own, v_rim, slab, t_own, t_rim, u_own, u_rim,
):
    x_taps = [weights[0, 16 - a] for a in range(17)]
    y_taps = [weights[1, 16 - a] for a in range(17)]
    base = 8 * side
    slide(s_own, base, t_own, x_taps, 8)
    slide(s_rim, base, t_rim, x_taps, 8)

    def back(x, carry):
        u_own[x] = along_rows(t_own, x, y_taps, 48)
        u_rim[x] = along_rows(t_rim, x, y_taps, 48)
        return carry

    lax.fori_loop(0, 8, back, 0)
    both = jnp.concatenate([u_own[...].reshape(384, LANES), u_rim[...].reshape(384, LANES)], axis=1)
    smeared = times(both, halves(gather[...]))
    planes = pl.ds(base, 8)
    for c, v, part in ((c_own, v_own, smeared[:, :LANES]), (c_rim, v_rim, smeared[:, LANES:])):
        coarse = c[pl.ds(at_c, 8), 8:56, :]
        v[...] = -0.5 * coarse * coarse + 0.5 / 3.0 * coarse * coarse * coarse + part.reshape(8, 48, LANES)
    corr[...] = v_own[:, 8:40, :]
    v_own[:, 0:8, :] += low[planes, 24:32, :]
    v_own[:, 8:40, :] += external[planes]
    v_own[:, 40:48, :] += high[planes, 24:32, :]
    for x in range(8):
        here = 16 + 2 * side + x // 4, slice(8 * (x // 2 % 2), 8 * (x // 2 % 2) + 8)
        for q in range(6):
            v_rim[x, 8 * q : 8 * q + 8, :] += unpack(right[here], left[here], 48 * (x % 2) + 8 * q, 8)

    lanes = lane_ids((8, LANES))
    edge, beyond = 4 * side, 4 - 4 * side
    rims = jnp.zeros((8, LANES), F32)
    for i in range(4):
        for q in range(5):
            slab[5 * i + q] = v_own[edge + i, 4 + 8 * q : 12 + 8 * q, :]
        for q in range(4):
            slab[20 + 4 * i + q] = v_own[beyond + i, 8 + 8 * q : 16 + 8 * q, :]
            at = 8 * (4 * i + q)
            these = (lanes >= at) & (lanes < at + 8)
            rims = jnp.where(these, pltpu.roll(v_rim[edge + i, 8 + 8 * q : 16 + 8 * q, :], (at + 4) % LANES, 1), rims)
    slab[36] = rims


def far_side(
    flags, weights, spread, gather, external, low, high, right, left, outer, o_low, o_high, o_right, o_left,
    own, rim, g_own, g_rim, s_own, s_rim, out_own, out_rim, s_all_own, s_all_rim, corr, v_own, v_rim, slab,
    e_own, e_rim, k_own, k_rim, c_own, c_rim, h_own, h_rim, t_own, t_rim, u_own, u_rim,
):
    upper = flags[0]
    below = 1 - upper
    fill(out_own, out_rim, 0, outer, o_low, o_high, o_right, o_left)
    along_z(out_own, out_rim, k_own, k_rim, 16 * upper, halves(spread[...]), 0)
    mine = pl.ds(16 * below, 16)
    k_own[mine] = g_own[...]
    k_rim[mine] = g_rim[...]
    for e, out, field in ((e_own, out_own, own), (e_rim, out_rim, rim)):
        e[pl.ds(8 * upper, 8)] = out[pl.ds(8 * below, 8)]
        e[pl.ds(8 * below, 8)] = field[pl.ds(24 * upper, 8)]
    for s_all, s in ((s_all_own, s_own), (s_all_rim, s_rim)):
        s_all[pl.ds(16 * below, 16)] = s[...]
    sources(
        weights, (e_own, e_rim), 0, k_own, k_rim, 0, s_all_own, s_all_rim, 16 * upper, c_own, c_rim, h_own, h_rim
    )
    potentials(
        upper, weights, gather, external, low, high, right, left, s_all_own, s_all_rim, c_own, c_rim, 8 * below,
        corr, v_own, v_rim, slab, t_own, t_rim, u_own, u_rim,
    )


def near_side(
    flags, weights, gather, external, low, high, right, left, s_own, s_rim, c_own, c_rim, far_corr,
    corr, v_own, v_rim, slab, near_corr, t_own, t_rim, u_own, u_rim,
):
    upper = flags[0]
    below = 1 - upper
    potentials(
        below, weights, gather, external, low, high, right, left, s_own, s_rim, c_own, c_rim, 8 * upper,
        near_corr, v_own, v_rim, slab, t_own, t_rim, u_own, u_rim,
    )
    corr[pl.ds(8 * below, 8)] = near_corr[...]
    corr[pl.ds(8 * upper, 8)] = far_corr[...]


def laplace(own, rim, x, count, start, rows, shifts, with_rim):
    planes = pl.ds(x, count)
    here = slice(start, start + rows)
    centers = own[planes, here, :], rim[planes, here, :]
    flat = [c.reshape(count * rows, LANES) for c in centers]
    shifted = times(jnp.concatenate(flat, axis=1), shifts)
    answers = []
    for ref in range(2 if with_rim else 1):
        field = (own, rim)[ref]
        part = shifted[:, LANES * ref : LANES * ref + LANES].reshape(count, rows, LANES)
        total = (1.0 + 0.5 * STEP * 3.0 * LAP_COEF[0]) * centers[ref] + part
        for k in range(1, 5):
            near = field[pl.ds(x + k, count), here, :] + field[pl.ds(x - k, count), here, :]
            near = near + (field[planes, start + k : start + k + rows, :] + field[planes, start - k : start - k + rows, :])
            total = total + (0.5 * STEP * LAP_COEF[k]) * near
        answers.append(total)
    return answers


def ring_shifts():
    gap = np.abs(np.arange(256)[:, None] - np.arange(256)[None, :])
    gap = np.minimum(gap, 256 - gap)
    matrix = np.zeros((256, 256), np.float32)
    for k in range(1, 5):
        matrix[gap == k] = 0.5 * STEP * LAP_COEF[k]
    return matrix


def first_step(flags, shifts, own, rim, out_own, out_rim, p_own, p_rim, e_own, e_rim):
    shift_halves = halves(shifts[...])
    upper = flags[0]
    for e, field, out in ((e_own, own, out_own), (e_rim, rim, out_rim)):
        e[pl.ds(16 * (1 - upper), 32)] = field[...]
        e[pl.ds(32 * upper, 16)] = out[...]

    def planes(k, carry):
        at = pl.ds(4 * k, 4)
        p_own[at], p_rim[at] = laplace(e_own, e_rim, 4 * k + 8, 4, 16, 48, shift_halves, True)
        return carry

    lax.fori_loop(0, 8, planes, 0)


def add_halo(slab, side, v_own, v_rim):
    lanes = lane_ids((8, LANES))
    edge, beyond = 4 + 20 * side, 28 * side
    empty = jnp.zeros((48, LANES), F32)
    for i in range(4):
        v_own[beyond + i] = empty
        v_rim[beyond + i] = empty
        v_own[edge + i] = empty
        v_rim[edge + i] = empty
        for q in range(5):
            v_own[edge + i, 4 + 8 * q : 12 + 8 * q, :] = slab[5 * i + q]
        for q in range(4):
            v_own[beyond + i, 8 + 8 * q : 16 + 8 * q, :] = slab[20 + 4 * i + q]
            rim = pltpu.roll(slab[36], (2 * LANES - 4 - 8 * (4 * i + q)) % LANES, 1)
            v_rim[edge + i, 8 + 8 * q : 16 + 8 * q, :] = jnp.where((lanes < 4) | (lanes >= LANES - 4), rim, 0.0)


def masks(flags, count, edge):
    rows = lax.broadcasted_iota(jnp.int32, (count, LANES), 0) - edge
    lanes = lane_ids((count, LANES))
    in_rows = (rows >= flags[3]) & (rows < flags[4])
    in_rim = ((lanes >= 64) & (flags[5] != 0)) | ((lanes < 64) & (flags[6] != 0))
    rows_one = jnp.where(in_rows, 1.0, 0.0)
    return rows_one, jnp.where(in_rim, rows_one, 0.0)


def steps(
    flags, shifts, p_own, p_rim, q_own, q_rim, at_q, v_own, v_rim, a_own, a_rim, b_own, b_rim, psi, one, two, three
):
    shift_halves = halves(shifts[...])
    last_halves = [m[:, :LANES] for m in shift_halves]

    def inside(x, edge):
        return jnp.where((x - edge >= flags[1]) & (x - edge < flags[2]), 1.0, 0.0)

    keep_own, keep_rim = masks(flags, 48, 8)

    def step_one(k, carry):
        x = one[0] + k
        keep = inside(x, 8)
        a_own[x] = (p_own[x] - STEP * v_own[x] * q_own[at_q + k, 16:64, :]) * (keep * keep_own)
        a_rim[x] = (p_rim[x] - STEP * v_rim[x] * q_rim[at_q + k, 16:64, :]) * (keep * keep_rim)
        return carry

    lax.fori_loop(0, one[1], step_one, 0, unroll=2)
    mid_own, mid_rim = masks(flags, 40, 4)

    def step_two(k, carry):
        x = two[0] + 4 * k
        at = pl.ds(x + 4, 4)
        fields = laplace(a_own, a_rim, x + 4, 4, 4, 40, shift_halves, True)
        for a, b, v, field, mask in (
            (a_own, b_own, v_own, fields[0], mid_own),
            (a_rim, b_rim, v_rim, fields[1], mid_rim),
        ):
            field = field - STEP * (v[at, 4:44, :] * a[at, 4:44, :])
            for i in range(4):
                b[x + i] = field[i] * (inside(x + i, 4) * mask)
        return carry

    lax.fori_loop(0, two[1] // 4, step_two, 0)

    def step_three(k, total):
        x = three[0] + 4 * k
        (field,) = laplace(b_own, b_rim, x + 4, 4, 4, 32, last_halves, False)
        field = field - STEP * (v_own[pl.ds(x + 8, 4), 8:40, :] * b_own[pl.ds(x + 4, 4), 4:36, :])
        psi[pl.ds(4 * k, 4)] = field
        return total + jnp.sum(field * field, axis=0)

    total = lax.fori_loop(0, three[1] // 4, step_three, jnp.zeros((32, LANES), F32))
    return jnp.sum(total, axis=0, keepdims=True)


def near_steps(
    flags, shifts, p_own, p_rim, q_own, q_rim, slab, v_far_own, v_far_rim, v_near_own, v_near_rim,
    a_kept_own, a_kept_rim, b_kept_own, b_kept_rim, psi, squares, v_own, v_rim, a_own, a_rim, b_own, b_rim,
):
    upper = flags[0]
    below = 1 - upper
    for v, far, near in ((v_own, v_far_own, v_near_own), (v_rim, v_far_rim, v_near_rim)):
        v[pl.ds(8 + 8 * upper, 8)] = far[...]
        v[pl.ds(8 + 8 * below, 8)] = near[...]
    add_halo(slab, below, v_own, v_rim)
    squares[...] = steps(
        flags, shifts, p_own, p_rim, q_own, q_rim, 8 * upper, v_own, v_rim, a_own, a_rim, b_own, b_rim, psi,
        (8 * below, 24), (8 * below, 16), (8 * below, 8),
    )
    a_kept_own[...] = a_own[pl.ds(8 + 8 * upper, 8)]
    a_kept_rim[...] = a_rim[pl.ds(8 + 8 * upper, 8)]
    b_kept_own[...] = b_own[8:16]
    b_kept_rim[...] = b_rim[8:16]


def far_steps(
    flags, shifts, p_own, p_rim, q_own, q_rim, slab, v_far_own, v_far_rim, near_squares,
    a_kept_own, a_kept_rim, b_kept_own, b_kept_rim, psi, squares, v_own, v_rim, a_own, a_rim, b_own, b_rim,
):
    upper = flags[0]
    below = 1 - upper
    v_own[pl.ds(8 + 8 * upper, 8)] = v_far_own[...]
    v_rim[pl.ds(8 + 8 * upper, 8)] = v_far_rim[...]
    a_own[pl.ds(8 + 8 * upper, 8)] = a_kept_own[...]
    a_rim[pl.ds(8 + 8 * upper, 8)] = a_kept_rim[...]
    b_own[8:16] = b_kept_own[...]
    b_rim[8:16] = b_kept_rim[...]
    add_halo(slab, upper, v_own, v_rim)
    squares[...] = near_squares[...] + steps(
        flags, shifts, p_own, p_rim, q_own, q_rim, 8 * below, v_own, v_rim, a_own, a_rim, b_own, b_rim, psi,
        (24 * upper, 8), (16 * upper, 8), (8 * upper, 8),
    )


def scale(count, flags, rows, near_psi, far_psi, out):
    total = jnp.sum(rows[...].reshape(-1, LANES), axis=0, keepdims=True)
    total = jnp.sum(total, axis=1, keepdims=True)
    factor = lax.rsqrt(total / count + 1e-06)
    upper = flags[0]
    out[pl.ds(8 * (1 - upper), 8)] = near_psi[...] * factor[None]
    out[pl.ds(8 * upper, 8)] = far_psi[...] * factor[None]


def swap_far(planes):
    count = lax.axis_size(GX)
    return lax.ppermute(planes, GX, [p for k in range(1, count - 1, 2) for p in ((k, k + 1), (k + 1, k))])


def swap_near(planes):
    return lax.ppermute(planes, GX, [(k, k ^ 1) for k in range(lax.axis_size(GX))])


def shift(head, tail, axis):
    ends = lax.axis_size(axis) - 1
    low = lax.ppermute(tail, axis, [(i, i + 1) for i in range(ends)])
    high = lax.ppermute(head, axis, [(i + 1, i) for i in range(ends)])
    return low, high


def spread(row, axes):
    count = lax.axis_size(axes)
    return lax.all_to_all(jnp.broadcast_to(row[None], (count, *row.shape)), axes, 0, 0, tiled=True)


def shards(wave, external, weights):
    at = [lax.axis_index(axis) for axis in (GX, "gy", "gz")]
    last = [at[d] == lax.axis_size(axis) - 1 for d, axis in enumerate((GX, "gy", "gz"))]
    far = 1 << 20
    flags = jnp.stack(
        [
            lax.axis_index("gx_2"),
            jnp.where(at[0] == 0, 0, -far),
            jnp.where(last[0], wave.shape[0], far),
            jnp.where(at[1] == 0, 0, -far),
            jnp.where(last[1], wave.shape[1], far),
            jnp.where(at[2] == 0, 0, 1),
            jnp.where(last[2], 0, 1),
        ]
    ).astype(jnp.int32)
    block = wave.shape
    outer = swap_far(wave)
    head, tail, same = call(cut, [block] * 3, [], wave, external)
    inner = swap_near(same)
    low, high = shift(head, tail, "gy")
    smear_z, gather_z, token = call(bands, [(256, 256)] * 2 + [(8, LANES)], [], weights, scalars=1, flops=5 * 10**9)
    first, final, rows = call(
        pack_both,
        [(20, 16, LANES)] * 2 + [(16, 48, LANES)],
        [],
        wave, external, low, high,
        after=(inner, token),
    )
    left, right = shift(first, final, "gz")
    i_rows = swap_near(rows)
    o_low, o_high = shift(*call(cut_outer, [(16, 24, LANES)] * 2, [], outer, after=(first, final)), "gy")
    first, final, sides = call(
        pack_outer, [(16, 16, LANES)] * 2 + [(16, 32, LANES)], [], outer, o_low, o_high, right, left
    )
    o_left, o_right = shift(first, final, "gz")
    i_sides = swap_near(sides)

    def twice(*shape):
        return [(*shape, LANES)] * 2

    own, rim, g_own, g_rim, s_own, s_rim, c_own, c_rim = call(
        prepare,
        twice(32, 80) + twice(16, 80) + twice(16, 64) + twice(16, 64),
        twice(32, 80) + twice(16, 80),
        flags, weights, smear_z, wave, low, high, right, left, inner, i_rows, i_sides,
        scalars=2,
    )
    halo = (low, high, right, left)
    out_own, out_rim, s_own, s_rim, far_corr, v_far_own, v_far_rim, outward = call(
        far_side,
        twice(16, 80) + twice(32, 64) + [(8, 32, LANES)] + twice(8, 48) + [(37, 8, LANES)],
        twice(16, 80) + twice(32, 80) + twice(16, 64) + twice(16, 80) + twice(8, 64) + twice(8, 48),
        flags, weights, smear_z, gather_z, external, *halo, outer, o_low, o_high, o_right, o_left,
        own, rim, g_own, g_rim, s_own, s_rim,
        scalars=2,
    )
    v_outer = swap_far(outward)
    shifts = jnp.asarray(ring_shifts())

    def beside(*args):
        corr, v_near_own, v_near_rim, inward = call(
            near_side,
            [block] + twice(8, 48) + [(37, 8, LANES)],
            [(8, 32, LANES)] + twice(8, 64) + twice(8, 48),
            flags, weights, gather_z, external, *halo, s_own, s_rim, c_own, c_rim, far_corr,
            scalars=2,
        )
        v_inner = swap_near(inward)
        p_own, p_rim = call(
            first_step, twice(32, 48), twice(48, 80), flags, shifts, own, rim, out_own, out_rim, scalars=1
        )
        return corr, v_near_own, v_near_rim, v_inner, p_own, p_rim

    def nothing(*args):
        shapes = [block, *twice(8, 48), (37, 8, LANES), *twice(32, 48)]
        return tuple(jnp.zeros(shape, F32) for shape in shapes)

    corr, v_near_own, v_near_rim, v_inner, p_own, p_rim = lax.cond(flags[0] >= 0, beside, nothing)
    scratch = twice(32, 48) * 2 + twice(24, 40)
    *kept, near_psi, squares = call(
        near_steps, twice(8, 48) + twice(8, 40) + [(8, 32, LANES), (1, LANES)], scratch,
        flags, shifts, p_own, p_rim, own, rim, v_inner, v_far_own, v_far_rim, v_near_own, v_near_rim,
        scalars=1,
    )
    far_psi, squares = call(
        far_steps, [(8, 32, LANES), (1, LANES)], scratch,
        flags, shifts, p_own, p_rim, out_own, out_rim, v_outer, v_far_own, v_far_rim, squares, *kept,
        scalars=1,
    )
    rows = spread(jnp.sum(spread(squares, RINGS[0]), axis=0), RINGS[1])
    count = float(wave.size * lax.axis_size(GX) * lax.axis_size("gy") * lax.axis_size("gz"))
    (wave_next,) = call(functools.partial(scale, count), [block], [], flags, rows, near_psi, far_psi, scalars=1)
    return (wave_next, corr)


def solution(mesh):
    torus = Mesh(
        mesh.devices.reshape(4, 2, 2, mesh.shape["gy"], mesh.shape["gz"]),
        ("gx_0", "gx_1", "gx_2", "gy", "gz"),
    )
    placed = (P(GX, "gy", "gz"), P(GX, "gy", "gz"), P())
    return jax.shard_map(
        shards,
        mesh=torus,
        in_specs=placed,
        out_specs=(P(GX, "gy", "gz"), P(GX, "gy", "gz")),
        check_vma=False,
    )
```
